128 devices in a mesh: pipe: 16 (over y, z_lo, core), tensor: 4 (over x), dp: 2 (over z_hi).
Axes of the slice: x: 4, y: 4, z: 4 (z_hi: 2, z_lo: 2; z = z_hi * 2 + z_lo), core: 2. Of those that a mesh axis runs over, the one named last changes fastest.
Arguments:
- hidden: bfloat16 [16, 256, 8192], P('pipe', 'dp', 'tensor'), may hold values from -3 to 3
- section_cotangent: bfloat16 [16, 256, 8192], P('pipe', 'dp', 'tensor'), may hold values from -3 to 3
- norm_gain: float32 [8192], P('tensor'), may hold values from 0.5 to 1.5
- head: bfloat16 [65536, 8192], P(('pipe', 'tensor', 'dp')), may hold values from -16 to 16
- labels: int32 [256], P('dp'), may hold values from 0 to 65535
- loss_mask: int32 [256], P('dp'), may hold values from 0 to 1
- exit_on: int32 [16], replicated, may hold values from 0 to 1, as said below
Outputs:
- head_grad: bfloat16 [65536, 8192], P(('pipe', 'tensor', 'dp'))
- residual_grad: bfloat16 [16, 256, 8192], P('pipe', 'dp', 'tensor')
- gain_grad: float32 [8192], P('tensor')
The draws below stay inside these ranges and needn't reach their ends.
Inputs may be any that keep to these rules, and one draw needn't show every extreme that they name: `exit_on`: exactly 2 entries are 1.
All inputs are finite; a program needn't handle non-finite values.
Results may differ from the reference program's by a relative error of at most 0.0045.
The reference program's roundings to bfloat16 on the way count: a program that leaves them out, or rounds other values in their place, can miss the bound.
Values may be sent and summed in bfloat16 or wider, within the bound.
No kernel may reach another device: no remote copies, remote signals or barrier semaphores. Data moves between devices by JAX's collectives and lax.ppermute only.
A program may use at most 128 MiB of HBM per device.

```python
import math
import jax
import jax.numpy as jnp
import numpy as np
from jax import lax

D = 8192
E_ON = 2
SECTIONS = 16
TOKENS = 256
VOCAB = 65536


def anchor_rows(key):
    return jax.random.uniform(key, (4, D), jnp.float32, -1.732, 1.732)


def draw_hidden(key, part):
    anchors = anchor_rows(key)
    key = jax.random.fold_in(key, 3)
    key_mix = jax.random.fold_in(key, 13)
    key_pos = jax.random.fold_in(key, 31)
    base = jnp.clip(jax.random.normal(key, (SECTIONS, TOKENS, D), jnp.float32), -6.0, 6.0)
    mixing = jax.random.uniform(key_mix, (SECTIONS, TOKENS, 1), jnp.float32, 0.7, 1.0)
    aligned_count = max(2, TOKENS // 32)
    positions = jax.random.permutation(key_pos, TOKENS)[:aligned_count].astype(jnp.int32)
    aligned_flags = jnp.zeros((TOKENS,), jnp.float32).at[positions].set(1.0)
    anchor_pick = jnp.zeros((TOKENS,), jnp.int32).at[positions].set(jnp.arange(aligned_count, dtype=jnp.int32) % 4)
    aligned = aligned_flags[None, :, None]
    target = anchors[anchor_pick][None, :, :]
    blended = mixing * target + (1.0 - mixing) * base
    mixed_rows = aligned * blended + (1.0 - aligned) * base
    return jnp.clip(0.05 * mixed_rows, -3.0, 3.0).astype(jnp.bfloat16)


def draw_head(key, part):
    anchors = anchor_rows(key)
    key = jax.random.fold_in(key, 5)
    key_ids = jax.random.fold_in(key, 37)
    spread = 3.0 / math.sqrt(D)
    planted_ids = jnp.arange(8, dtype=jnp.int32)
    planted_rows = jax.random.permutation(key_ids, VOCAB)[:8].astype(jnp.int32)
    strength = jnp.array([130.0, 260.0, 400.0, 560.0], jnp.float32)[planted_ids // 2] + 2.0 * (planted_ids % 2).astype(jnp.float32)
    planted = strength[:, None] * anchors[planted_ids // 2] / D
    scaled = spread * jnp.clip(jax.random.normal(key, (VOCAB, D), jnp.float32), -6.0, 6.0)
    return jnp.clip(scaled.at[planted_rows].set(planted), -16.0, 16.0).astype(jnp.bfloat16)


def draw_loss_mask(key, part):
    key = jax.random.fold_in(key, 19)
    key_pos = jax.random.fold_in(key, 23)
    levels = jax.random.randint(key, (TOKENS,), 0, 4)
    mask = (levels > 0).astype(jnp.int32)
    zero_at = jax.random.randint(key_pos, (), 0, TOKENS)
    return mask.at[zero_at].set(0)


def draw_exit_on(key, part):
    key = jax.random.fold_in(key, 7)
    shuffled = jax.random.permutation(key, SECTIONS)
    picked = shuffled[:E_ON]
    return jnp.zeros((SECTIONS,), jnp.int32).at[picked].set(1)


def place_ends(entries, rng, smallest, top_value):
    index_at = [jax.random.randint(jax.random.fold_in(rng, axis), (), 0, length) for axis, length in enumerate(entries.shape)]
    widest = entries.shape.index(max(entries.shape))
    neighbour = index_at[:widest] + [(index_at[widest] + 1) % entries.shape[widest]] + index_at[widest + 1:]
    return entries.at[tuple(index_at)].set(smallest).at[tuple(neighbour)].set(top_value)


def block_scale(own_key, dims, cuts, smallest, top_value):
    loudness, own = 1.0, jax.random.fold_in(own_key, 6)
    for dim, parts in cuts:
        steps = jnp.exp(jax.random.uniform(jax.random.fold_in(own, dim), (parts,), jnp.float32, smallest / len(cuts), top_value / len(cuts)))
        loudness = loudness * jnp.repeat(steps, dims[dim] // parts).reshape([-1 if axis == dim else 1 for axis in range(len(dims))])
    return loudness


def rank_table(amount, lean):
    weights = [(1 << 20) // math.isqrt(rank ** lean) + 1 for rank in range(1, amount + 1)]
    scale = 1 + sum(weights) // (1 << 30)
    return np.cumsum(np.array([max(1, weight // scale) for weight in weights]))


def ranked(key, dims, amount, lean):
    grid = rank_table(amount, lean)
    lot = jax.random.randint(jax.random.fold_in(key, 1), dims, 0, int(grid[amount - 1]))
    rank = jnp.searchsorted(jnp.asarray(grid, jnp.int32), lot, side="right")
    return jax.random.permutation(jax.random.fold_in(key, 2), amount)[rank].astype(jnp.int32)


def gaussian(own_key, shape, scale, bound, split=(), kind=jnp.bfloat16):
    values = scale * jax.random.normal(own_key, shape, jnp.float32)
    if split:
        values = values * block_scale(own_key, shape, split, -0.22, 0.18)
    return jnp.clip(values, -bound, bound).astype(kind)


def setup_inputs(seed: int = 0) -> dict:
    key_list = jax.random.split(jax.random.key(seed), 8)
    return {
        "hidden": draw_hidden(jax.random.fold_in(key_list[7], 71), 0),
        "section_cotangent": gaussian(key_list[1], (SECTIONS, TOKENS, D), 0.5, 3.0, ((0, 16), (1, 2), (2, 4))),
        "norm_gain": jnp.clip(1.0 + 0.1 * jax.random.normal(key_list[2], (D,), jnp.float32), 0.5, 1.5),
        "head": draw_head(jax.random.fold_in(key_list[7], 71), 0),
        "labels": place_ends(ranked(key_list[4], (TOKENS,), VOCAB, 2), jax.random.fold_in(key_list[4], 3), 0, VOCAB - 1).astype(jnp.int32),
        "loss_mask": draw_loss_mask(jax.random.fold_in(key_list[7], 71), 0),
        "exit_on": draw_exit_on(jax.random.fold_in(key_list[7], 71), 0),
    }


NORM_EPS = 1e-05

def reference(hidden, section_cotangent, norm_gain, head, labels, loss_mask, exit_on):
    section_ids = jnp.arange(SECTIONS, dtype=jnp.int32)
    enabled = jnp.argsort(1 - exit_on, stable=True)[:E_ON].astype(jnp.int32)
    scores = (exit_on * (section_ids + 1)).astype(jnp.float32)
    weights = scores / jnp.sum(scores)
    widened = hidden.astype(jnp.float32)
    inverse_rms = lax.rsqrt(lax.optimization_barrier(jnp.mean(widened * widened, axis=-1, keepdims=True)) + NORM_EPS)
    unit_rows = widened * inverse_rms
    normed = (unit_rows * norm_gain).astype(jnp.bfloat16)
    chosen = normed[enabled].reshape(E_ON * TOKENS, D)
    logits = jnp.dot(chosen, head.T, preferred_element_type=jnp.float32)
    row_top = lax.optimization_barrier(jnp.max(logits, axis=1, keepdims=True))
    log_total = row_top + jnp.log(lax.optimization_barrier(jnp.sum(jnp.exp(logits - row_top), axis=1, keepdims=True)))
    softmax_rows = jnp.exp(logits - log_total)
    vocab_ids = jnp.arange(VOCAB, dtype=jnp.int32)
    label_rows = jnp.tile(labels, E_ON)
    onehot = (label_rows[:, None] == vocab_ids[None, :]).astype(jnp.float32)
    row_weights = (weights[enabled][:, None] * loss_mask[None, :].astype(jnp.float32)).reshape(-1)
    dlogits = (row_weights[:, None] * (softmax_rows - onehot)).astype(jnp.bfloat16)
    head_grad = jnp.dot(dlogits.T, chosen, preferred_element_type=jnp.float32).astype(jnp.bfloat16)
    exit_part = jnp.dot(dlogits, head, preferred_element_type=jnp.float32).reshape(E_ON, TOKENS, D)
    normed_grad = jnp.zeros((SECTIONS, TOKENS, D), jnp.float32).at[enabled].set(exit_part)
    gated_grad = normed_grad * norm_gain
    inner_sums = lax.optimization_barrier(jnp.mean(gated_grad * unit_rows, axis=-1, keepdims=True))
    exit_grad = inverse_rms * (gated_grad - unit_rows * inner_sums)
    from_next = jnp.concatenate([section_cotangent[1:], jnp.zeros_like(section_cotangent[:1])], axis=0)
    residual_grad = (exit_grad + from_next.astype(jnp.float32)).astype(jnp.bfloat16)
    gain_grad = lax.optimization_barrier(jnp.sum(normed_grad * unit_rows, axis=(0, 1)))
    return (head_grad, residual_grad, gain_grad)
```

```python
import functools

import jax
import jax.numpy as jnp
import numpy as np
from jax import lax
from jax.experimental import pallas as pl
from jax.experimental.pallas import tpu as pltpu
from jax.sharding import Mesh, PartitionSpec as P

NORM_EPS = 1e-05
AXES = ("y", "zl", "c", "x", "zh")
SIZES = (4, 2, 2, 4, 2)
CHIPS = ("y", "zl", "x", "zh")
PIPE = ("y", "zl", "c")
F32, BF16 = jnp.float32, jnp.bfloat16
NT = (((1,), (1,)), ((), ()))
NN = (((1,), (0,)), ((), ()))


def route(step):
    pairs = []
    for source in range(128):
        y, zl, c, x, zh = (int(i) for i in np.unravel_index(source, SIZES))
        there = step(y, 2 * zh + zl, c, x)
        if there is not None:
            y, z, c, x = there[0] % 4, there[1] % 4, there[2] % 2, there[3] % 4
            pairs.append((source, int(np.ravel_multi_index((y, z % 2, c, x, z // 2), SIZES))))
    return pairs


def move(block, step):
    return lax.ppermute(block, AXES, route(step))


def other_core(block):
    return move(block, lambda y, z, c, x: (y, z, 1 - c, x))


def logits_kernel(cols, own, other, head, logits, lse, total):
    step = pl.program_id(0)

    @pl.when(step == 0)
    def _():
        total[...] = lax.dot_general(head[...], own[...], NT, preferred_element_type=F32)

    @pl.when((step > 0) & (step < 4))
    def _():
        total[...] += lax.dot_general(head[...], own[...], NT, preferred_element_type=F32)

    @pl.when(step >= 4)
    def _():
        total[...] += lax.dot_general(head[...], other[...], NT, preferred_element_type=F32)

    @pl.when(step == 7)
    def _():
        values = total[...]
        logits[...] = values
        top = jnp.max(values, axis=0, keepdims=True)
        lse[...] = top + jnp.log(jnp.sum(jnp.exp(values - top), axis=0, keepdims=True))


def logits_call(cols, own, other, head):
    return pl.pallas_call(
        logits_kernel,
        grid_spec=pltpu.PrefetchScalarGridSpec(
            num_scalar_prefetch=1,
            grid=(8,),
            in_specs=[
                pl.BlockSpec((512, 1024), lambda s, cols: (0, jnp.minimum(s, 3))),
                pl.BlockSpec((512, 1024), lambda s, cols: (0, jnp.maximum(s - 4, 0))),
                pl.BlockSpec((512, 1024), lambda s, cols: (0, cols[s])),
            ],
            out_specs=[
                pl.BlockSpec((512, 512), lambda s, cols: (0, 0)),
                pl.BlockSpec((1, 512), lambda s, cols: (0, 0)),
            ],
            scratch_shapes=[pltpu.VMEM((512, 512), F32)],
        ),
        out_shape=[jax.ShapeDtypeStruct((512, 512), F32), jax.ShapeDtypeStruct((1, 512), F32)],
        compiler_params=pltpu.CompilerParams(vmem_limit_bytes=32 << 20),
    )(cols, own, other, head)


def dlogits_kernel(start, logits, parts, labels, weights, dlogits):
    lse = parts[...]
    top = jnp.max(lse, axis=0, keepdims=True)
    log_total = top + jnp.log(jnp.sum(jnp.exp(lse - top), axis=0, keepdims=True))
    probs = jnp.exp(logits[...] - log_total)
    ids = start[0] + lax.broadcasted_iota(jnp.int32, (512, 512), 0)
    hot = jnp.where(ids == labels[...], 1.0, 0.0)
    dlogits[...] = (weights[...] * (probs - hot)).astype(BF16)


def dlogits_call(start, logits, parts, labels, weights):
    vmem = pl.BlockSpec(memory_space=pltpu.VMEM)
    return pl.pallas_call(
        dlogits_kernel,
        in_specs=[pl.BlockSpec(memory_space=pltpu.SMEM), vmem, vmem, vmem, vmem],
        out_specs=vmem,
        out_shape=jax.ShapeDtypeStruct((512, 512), BF16),
        compiler_params=pltpu.CompilerParams(vmem_limit_bytes=32 << 20),
    )(start, logits, parts, labels, weights)


def back_kernel(cols, dlogits, head, out, turned):
    @pl.when(pl.program_id(0) == 0)
    def _():
        turned[...] = dlogits[...].T

    out[...] = jnp.dot(turned[...], head[...], preferred_element_type=F32).astype(BF16)


def back_call(cols, dlogits, head):
    return pl.pallas_call(
        back_kernel,
        grid_spec=pltpu.PrefetchScalarGridSpec(
            num_scalar_prefetch=1,
            grid=(4,),
            in_specs=[
                pl.BlockSpec((512, 512), lambda s, cols: (0, 0)),
                pl.BlockSpec((512, 1024), lambda s, cols: (0, cols[s])),
            ],
            out_specs=pl.BlockSpec((512, 1024), lambda s, cols: (0, s)),
            scratch_shapes=[pltpu.VMEM((512, 512), BF16)],
        ),
        out_shape=jax.ShapeDtypeStruct((512, 4096), BF16),
        cost_estimate=pl.CostEstimate(flops=2 * 512 * 512 * 4096, bytes_accessed=9 << 20, transcendentals=0),
        compiler_params=pltpu.CompilerParams(vmem_limit_bytes=32 << 20),
    )(cols, dlogits, head)


def head_kernel(cols, dlogits, own, other, out):
    @pl.when(pl.program_id(0) < 4)
    def _():
        out[...] = jnp.dot(dlogits[...], own[...], preferred_element_type=F32).astype(BF16)

    @pl.when(pl.program_id(0) >= 4)
    def _():
        out[...] = jnp.dot(dlogits[...], other[...], preferred_element_type=F32).astype(BF16)


def head_call(cols, dlogits, own, other):
    return pl.pallas_call(
        head_kernel,
        grid_spec=pltpu.PrefetchScalarGridSpec(
            num_scalar_prefetch=1,
            grid=(8,),
            in_specs=[
                pl.BlockSpec((512, 512), lambda s, cols: (0, 0)),
                pl.BlockSpec((512, 1024), lambda s, cols: (0, jnp.minimum(s, 3))),
                pl.BlockSpec((512, 1024), lambda s, cols: (0, jnp.maximum(s - 4, 0))),
            ],
            out_specs=pl.BlockSpec((512, 1024), lambda s, cols: (0, cols[s])),
        ),
        out_shape=jax.ShapeDtypeStruct((512, 8192), BF16),
        cost_estimate=pl.CostEstimate(flops=2 * 512 * 512 * 8192, bytes_accessed=17 << 20, transcendentals=0),
        compiler_params=pltpu.CompilerParams(vmem_limit_bytes=32 << 20),
    )(cols, dlogits, own, other)


def local(hidden, section_cotangent, norm_gain, head, labels, loss_mask, exit_on):
    core, x, zh = lax.axis_index("c"), lax.axis_index("x"), lax.axis_index("zh")
    device = lax.axis_index(AXES)

    from_next = move(section_cotangent, lambda y, z, c, x: back_one(y, z, c, x))
    token_info = jnp.stack([labels, loss_mask])
    other_info = move(token_info, lambda y, z, c, x: (y, z + 2, c, x))
    half = lax.dynamic_slice_in_dim(norm_gain.reshape(2, 8, 128), core, 1, 0)
    turns = [half] + [move(half, lambda y, z, c, x, k=k: (y, z, c, x + k)) for k in (1, 2, 3)]
    ring = jnp.concatenate(turns[::-1], axis=0)
    gain = lax.dynamic_slice_in_dim(jnp.concatenate([ring, ring], axis=0), (3 - x) % 4, 4, 0)

    section_ids = jnp.arange(16, dtype=jnp.int32)
    first = jnp.min(jnp.where(exit_on == 1, section_ids, 16))
    second = jnp.max(jnp.where(exit_on == 1, section_ids, -1))
    scores = jnp.stack([first + 1, second + 1]).astype(F32)
    weights = scores / jnp.sum(scores)

    slots = hidden.reshape(4, 2, 4, 2, 2, 2, 8, 128).transpose(0, 1, 5, 2, 3, 4, 6, 7).reshape(128, 16, 128)
    came = lax.all_to_all(slots, AXES, 0, 0, tiled=True).reshape(16, 4, 2, 2, 8, 128)
    picked = jnp.stack([lax.dynamic_index_in_dim(came, s, 0, False) for s in (first, second)])
    rows = picked.astype(F32)
    squares = jnp.sum(rows * rows, axis=(1, 4, 5))
    squares = squares + other_core(squares)
    inverse_rms = lax.rsqrt(squares / 8192 + NORM_EPS)[:, None, :, :, None, None]
    unit = rows * inverse_rms
    spread_gain = gain[None, :, None, None]
    normed = (unit * spread_gain).astype(BF16)

    block = normed.transpose(0, 2, 3, 1, 4, 5).reshape(1, 8, 4096)
    own = lax.all_to_all(jnp.broadcast_to(block, (64, 8, 4096)), CHIPS, 0, 0, tiled=True).reshape(512, 4096)
    other = other_core(own)
    own_cols = jnp.arange(4, dtype=jnp.int32) * 2 + core
    other_cols = jnp.arange(4, dtype=jnp.int32) * 2 + 1 - core
    cols = jnp.concatenate([own_cols, other_cols])
    logits, lse = logits_call(cols, own, other, head)

    parts = lax.all_to_all(jnp.broadcast_to(lse.reshape(1, 4, 128), (128, 4, 128)), AXES, 0, 0, tiled=True)
    both = jnp.where(zh == 0, jnp.stack([token_info, other_info]), jnp.stack([other_info, token_info]))
    by_row = jnp.broadcast_to(
        both.reshape(2, 2, 64, 2).transpose(1, 2, 0, 3)[:, :, None], (2, 64, 2, 2, 2)
    )
    row_weights = weights[None, :, None, None] * by_row[1].astype(F32)
    dlogits = dlogits_call(
        (device * 512).reshape(1), logits, parts.reshape(128, 512), by_row[0].reshape(1, 512), row_weights.reshape(1, 512)
    )

    sent = back_call(other_cols, dlogits, head)
    got = other_core(sent)
    kept = back_call(own_cols, dlogits, head)
    head_grad = head_call(cols, dlogits, own, other)
    chip_sum = (kept.astype(F32) + got.astype(F32)).astype(BF16).reshape(64, 8, 4096)
    terms = lax.all_to_all(chip_sum, CHIPS, 0, 0, tiled=True)
    grad = jnp.sum(terms.astype(F32), axis=0).reshape(2, 2, 2, 4, 8, 128).transpose(0, 3, 1, 2, 4, 5)

    gated = grad * spread_gain
    inner = jnp.sum(gated * unit, axis=(1, 4, 5))
    inner = inner + other_core(inner)
    exit_grad = inverse_rms * (gated - unit * (inner / 8192)[:, None, :, :, None, None])
    gain_part = jnp.sum(grad * unit, axis=(0, 2, 3))
    high = gain_part.astype(BF16)
    low = (gain_part - high.astype(F32)).astype(BF16)
    ids = section_ids[:, None, None, None, None, None]
    placed = jnp.where(ids == first, exit_grad[0], jnp.where(ids == second, exit_grad[1], 0.0)).astype(BF16)
    gains = jnp.broadcast_to(jnp.stack([high, low], axis=1)[None, :, None], (16, 4, 2, 2, 8, 128))
    slots = jnp.concatenate([placed, gains], axis=3).reshape(128, 32, 128)
    came = lax.all_to_all(slots, AXES, 0, 0, tiled=True).reshape(4, 2, 2, 4, 2, 4, 8, 128)
    exits = came[:, :, :, :, :, :2].transpose(0, 1, 3, 4, 5, 2, 6, 7).reshape(128, 2048)
    gain_grad = jnp.sum(came[:, :, :, :, :, 2:].astype(F32), axis=(0, 1, 3, 4, 5)).reshape(2048)
    residual_grad = (exits.astype(F32) + from_next[0].astype(F32)).astype(BF16)[None]
    return head_grad, residual_grad, gain_grad


def back_one(y, z, c, x):
    section = (y * 2 + z % 2) * 2 + c - 1
    return None if section < 0 else (section // 4, z // 2 * 2 + section // 2 % 2, section % 2, x)


def solution(mesh):
    fine = Mesh(mesh.devices.reshape(SIZES), AXES)
    in_specs = (
        P(PIPE, "zh", "x"),
        P(PIPE, "zh", "x"),
        P("x"),
        P(AXES, None),
        P("zh"),
        P("zh"),
        P(),
    )
    out_specs = (P(AXES, None), P(PIPE, "zh", "x"), P("x"))
    return jax.shard_map(local, mesh=fine, in_specs=in_specs, out_specs=out_specs, check_vma=False)
```

```python
import functools

import jax
import jax.numpy as jnp
import numpy as np
from jax import lax
from jax.experimental import pallas as pl
from jax.experimental.pallas import tpu as pltpu
from jax.sharding import Mesh, PartitionSpec as P

NORM_EPS = 1e-05
AXES = ("y", "zl", "c", "x", "zh")
SIZES = (4, 2, 2, 4, 2)
CHIPS = ("x", "y", "zl", "zh")
PIPE = ("y", "zl", "c")
F32, BF16 = jnp.float32, jnp.bfloat16
NT = (((1,), (1,)), ((), ()))
LIMIT = 16 << 20
COLOURS = [(x + 2 * y + 3 * (2 * zh + zl)) % 4 for x in range(4) for y in range(4) for zl in range(2) for zh in range(2)]


def route(step):
    pairs = []
    for source in range(128):
        y, zl, c, x, zh = (int(i) for i in np.unravel_index(source, SIZES))
        there = step(y, 2 * zh + zl, c, x)
        if there is not None:
            y, z, c, x = there[0] % 4, there[1] % 4, there[2] % 2, there[3] % 4
            pairs.append((source, int(np.ravel_multi_index((y, z % 2, c, x, z // 2), SIZES))))
    return pairs


def move(block, step):
    return lax.ppermute(block, AXES, route(step))


def other_core(block):
    return move(block, lambda y, z, c, x: (y, z, 1 - c, x))


def to_colour(block, away):
    if away == 1:
        return move(block, lambda y, z, c, x: (y, z - 1, c, x) if c else (y, z, c, x + 1))
    if away == 3:
        return move(block, lambda y, z, c, x: (y, z + 1, c, x) if c else (y, z, c, x - 1))
    return move(block, lambda y, z, c, x: (y - 1 if c else y + 1, z, c, x))


def back_one(y, z, c, x):
    section = (y * 2 + z % 2) * 2 + c - 1
    return None if section < 0 else (section // 4, z // 2 * 2 + section // 2 % 2, section % 2, x)


def call(kernel, scalars, operands, outs, flops=0, moved=1 << 20):
    vmem = pl.BlockSpec(memory_space=pltpu.VMEM)
    smem = [] if scalars is None else [pl.BlockSpec(memory_space=pltpu.SMEM)]
    held = [pltpu.with_memory_space_constraint(o, pltpu.VMEM) for o in operands]
    return pl.pallas_call(
        kernel,
        in_specs=smem + [vmem] * len(operands),
        out_specs=[vmem] * len(outs),
        out_shape=[(jax.ShapeDtypeStruct if place else pltpu.VMEM)(shape, kind) for shape, kind, *place in outs],
        cost_estimate=pl.CostEstimate(flops=flops, bytes_accessed=moved, transcendentals=0),
        compiler_params=pltpu.CompilerParams(vmem_limit_bytes=LIMIT),
    )(*([] if scalars is None else [scalars]), *held)


def columns(tint, t, away):
    return pl.ds(pl.multiple_of(t * 2048 + tint[away] * 512, 512), 512)


def slots_kernel(rows, out):
    wide = rows[...].astype(F32)
    squares = jnp.sum(wide * wide, axis=1, keepdims=True)
    high = squares.astype(BF16).astype(F32)
    middle = (squares - high).astype(BF16).astype(F32)
    low = squares - high - middle
    lane = lax.broadcasted_iota(jnp.int32, (16, 128), 1)
    extra = jnp.where(lane == 0, high, jnp.where(lane == 1, middle, jnp.where(lane == 2, low, 0.0))).astype(BF16)
    for chip, colour in enumerate(COLOURS):
        out[chip, :, :512] = rows[:, colour * 512 : (colour + 1) * 512]
        out[chip, :, 512:] = extra


def slots_call(rows):
    return call(slots_kernel, None, [rows], [((64, 16, 640), BF16, True)])[0]


def norm_kernel(came, gain, own, inverse_rms):
    for group in range(16):
        span = slice(group * 16, (group + 1) * 16)
        squares = sum(came[t * 16 + group, :, 512:].astype(F32) for t in range(4))
        inverse = lax.rsqrt(jnp.sum(squares, axis=1, keepdims=True) / 8192 + NORM_EPS)
        inverse_rms[span, :] = jnp.broadcast_to(inverse, (16, 128))
        for t in range(4):
            unit = came[t * 16 + group, :, :512].astype(F32) * inverse
            own[t, span, :] = (unit * gain[t : t + 1, :]).astype(BF16)


def norm_call(came, gain):
    return call(norm_kernel, None, [came, gain], [((4, 256, 512), BF16), ((256, 128), F32, True)], moved=2 << 20)


def add_up(tint, aways, head, blocks, total):
    def part(t):
        return sum(
            lax.dot_general(head[:, columns(tint, t, away)], block[t], NT, preferred_element_type=F32)
            for away, block in zip(aways, blocks)
        )

    total[...] = part(0)

    @pl.loop(1, 4)
    def _(t):
        total[...] += part(t)


def logits_kernel(aways, tint, head, *refs):
    add_up(tint, aways, head, refs[:-1], refs[-1])


def logits_call(tint, head, aways, blocks):
    flops = 2 * 512 * 256 * 2048 * len(aways)
    kernel = functools.partial(logits_kernel, aways)
    return call(kernel, tint, [head, *blocks], [((512, 256), F32)], flops, len(aways) << 21)[0]


def last_kernel(tint, head, block_1, block_2, block_3, early, ours, theirs, logits, lse, total):
    add_up(tint, (1, 2, 3), head, (block_1, block_2, block_3), total)
    logits[:, :256] = early[...] + ours[...]
    logits[:, 256:] = theirs[...] + total[...]
    values = logits[...]
    top = jnp.max(values, axis=0, keepdims=True)
    sums = top + jnp.log(jnp.sum(jnp.exp(values - top), axis=0, keepdims=True))
    quarters = [sums[:, i * 128 : (i + 1) * 128] for i in range(4)]
    in_order = jnp.concatenate(quarters, axis=0)
    swapped = jnp.concatenate(quarters[2:] + quarters[:2], axis=0)
    lse[...] = jnp.broadcast_to(jnp.where(tint[4] == 0, in_order, swapped)[None], (128, 4, 128))


def last_call(tint, head, blocks, early, ours, theirs):
    outs = [((512, 512), F32), ((128, 4, 128), F32, True), ((512, 256), F32)]
    return call(last_kernel, tint, [head, *blocks, early, ours, theirs], outs, 6 * 512 * 256 * 2048, 9 << 20)[:2]


def dlogits_kernel(place, logits, parts, labels, weights, turned, dlogits):
    lse = parts[...]
    top = jnp.max(lse, axis=0)
    log_total = top + jnp.log(jnp.sum(jnp.exp(lse - top[None]), axis=0))
    quarters = [log_total[i : i + 1] for i in range(4)]
    in_order = jnp.concatenate(quarters, axis=1)
    swapped = jnp.concatenate(quarters[2:] + quarters[:2], axis=1)
    probs = jnp.exp(logits[...] - jnp.where(place[1] == 0, in_order, swapped))
    ids = place[0] * 512 + lax.broadcasted_iota(jnp.int32, (512, 512), 0)
    hot = jnp.where(ids == labels[...], 1.0, 0.0)
    values = (weights[...] * (probs - hot)).astype(BF16)
    turned[...] = values
    dlogits[...] = values.T


def dlogits_call(place, logits, parts, labels, weights):
    outs = [((512, 512), BF16)] * 2
    return call(dlogits_kernel, place, [logits, parts, labels, weights], outs, moved=3 << 20)


def fetch_kernel(after, source, out, sem):
    copy = pltpu.make_async_copy(source, out, sem)
    copy.start()
    copy.wait()


def fetch(source, after):
    return pl.pallas_call(
        fetch_kernel,
        in_specs=[pl.BlockSpec(memory_space=pl.ANY)] * 2,
        out_specs=pl.BlockSpec(memory_space=pltpu.VMEM),
        out_shape=pltpu.VMEM(source.shape, source.dtype),
        scratch_shapes=[pltpu.SemaphoreType.DMA],
        cost_estimate=pl.CostEstimate(flops=0, bytes_accessed=8 << 20, transcendentals=0),
        compiler_params=pltpu.CompilerParams(vmem_limit_bytes=LIMIT),
    )(after, source)


def back_kernel(away, tint, dlogits, head, own, other):
    @pl.loop(0, 4)
    def _(t):
        value = jnp.dot(dlogits[...], head[:, columns(tint, t, away)], preferred_element_type=F32)
        own[t] = value[:256]
        other[t] = value[256:].astype(BF16)


def back_call(tint, dlogits, head, away):
    kernel = functools.partial(back_kernel, away)
    outs = [((4, 256, 512), F32), ((4, 256, 512), BF16)]
    return call(kernel, tint, [dlogits, head], outs, 2 * 512 * 512 * 2048, 4 << 20)


def head_kernel(tint, turned, *refs):
    out = refs[-1]
    for away in range(4):
        own, other = refs[away], refs[4 + away]
        value = jnp.dot(turned[:, :256], own[0], preferred_element_type=F32)
        value += jnp.dot(turned[:, 256:], other[0], preferred_element_type=F32)
        out[:, pl.ds(pl.multiple_of(tint[away] * 512, 512), 512)] = value.astype(BF16)


def head_call(tint, turned, own, other):
    block = pl.BlockSpec((1, 256, 512), lambda t, tint: (t, 0, 0))
    return pl.pallas_call(
        head_kernel,
        grid_spec=pltpu.PrefetchScalarGridSpec(
            num_scalar_prefetch=1,
            grid=(4,),
            in_specs=[pl.BlockSpec((512, 512), lambda t, tint: (0, 0))] + [block] * 8,
            out_specs=pl.BlockSpec((512, 2048), lambda t, tint: (0, t)),
        ),
        out_shape=jax.ShapeDtypeStruct((512, 8192), BF16),
        cost_estimate=pl.CostEstimate(flops=2 * 512 * 512 * 8192, bytes_accessed=17 << 20, transcendentals=0),
        compiler_params=pltpu.CompilerParams(vmem_limit_bytes=LIMIT),
    )(tint, turned, *own, *other)


def tail_kernel(terms, rows, inverse_rms, gain, gated, unit, inner, gain_part):
    sums = [None] * 4
    for chip, colour in enumerate(COLOURS):
        term = terms[chip].astype(F32)
        sums[colour] = term if sums[colour] is None else sums[colour] + term
    inverse = inverse_rms[:, :1]
    total = jnp.zeros((16, 1), F32)
    for colour, grad in enumerate(sums):
        span = slice(colour * 512, (colour + 1) * 512)
        ours = rows[:, span].astype(F32) * inverse
        scaled = grad * gain[:, span]
        unit[:, span] = ours
        gated[:, span] = scaled
        total += jnp.sum(scaled * ours, axis=1, keepdims=True)
        part = jnp.sum(grad * ours, axis=0, keepdims=True)
        for i in range(2):
            gain_part[colour * 2 + i : colour * 2 + i + 1, :] = part[:, i * 256 : (i + 1) * 256]
    inner[...] = jnp.broadcast_to(total, (16, 128))


def tail_call(terms, rows, inverse_rms, gain):
    outs = [((16, 2048), F32), ((16, 2048), F32), ((16, 128), F32), ((8, 256), F32)]
    return call(tail_kernel, None, [terms, rows, inverse_rms, gain], outs, moved=2 << 20)


def exit_kernel(chosen, gated, unit, inverse_rms, inner, inner_1, inner_2, inner_3, gain, gain_1, out):
    total = (inner[...] + inner_1[...] + inner_2[...] + inner_3[...])[:, :1] / 8192
    grad = inverse_rms[:, :1] * (gated[...] - unit[...] * total)
    sums = gain[...] + gain_1[...]
    high = sums.astype(BF16).astype(F32)
    low = sums - high
    for section in range(16):
        value = jnp.where(chosen[0] == section, grad[:8], jnp.where(chosen[1] == section, grad[8:], 0.0))
        out[section] = jnp.concatenate([value, high, low], axis=1).astype(BF16)


def exit_call(chosen, *operands):
    return call(exit_kernel, chosen, operands, [((16, 8, 2560), BF16, True)])[0]


def local(hidden, section_cotangent, norm_gain, head, labels, loss_mask, exit_on):
    core, x, y, zl, zh = (lax.axis_index(a) for a in ("c", "x", "y", "zl", "zh"))
    device = lax.axis_index(AXES).astype(jnp.int32)
    colour = (x + 2 * y + 3 * (2 * zh + zl)) % 4
    aways = (colour + jnp.arange(4, dtype=jnp.int32)) % 4
    tint = jnp.concatenate([aways, core.reshape(1)]).astype(jnp.int32)

    came = lax.all_to_all(hidden.reshape(16, 8, 2048), PIPE, 0, 0, tiled=True)
    section_ids = jnp.arange(16, dtype=jnp.int32)
    first = jnp.min(jnp.where(exit_on == 1, section_ids, 16))
    second = jnp.max(jnp.where(exit_on == 1, section_ids, -1))
    chosen = jnp.stack([first, second])
    scores = (chosen + 1).astype(F32)
    weights = scores / jnp.sum(scores)

    turns = [norm_gain] + [move(norm_gain, lambda y, z, c, x, k=k: (y, z, c, x + k)) for k in (1, 2, 3)]
    ring = jnp.stack(turns[::-1] * 2)
    gain = lax.dynamic_slice(ring, ((3 - x) % 4, colour * 512), (4, 512))
    came, gain = lax.optimization_barrier((came, gain))
    rows = jnp.concatenate([lax.dynamic_index_in_dim(came, s, 0, False) for s in (first, second)])
    token_info = jnp.stack([labels, loss_mask])
    other_info = move(token_info, lambda y, z, c, x: (y, z + 2, c, x))
    both = jnp.where(zh == 0, jnp.stack([token_info, other_info]), jnp.stack([other_info, token_info]))
    by_row = jnp.broadcast_to(
        both.reshape(2, 2, 4, 2, 2, 8).transpose(4, 1, 2, 3, 0, 5)[:, :, :, :, :, None], (2, 2, 4, 2, 2, 2, 8)
    )
    by_row = jnp.where(core == 0, by_row, by_row[::-1])
    row_labels = by_row[:, 0].reshape(1, 512)
    row_weights = (weights[:, None] * by_row[:, 1].astype(F32)).reshape(1, 512)

    quarter = lax.all_to_all(slots_call(rows), CHIPS, 0, 0, tiled=True)
    quarter, row_labels, row_weights = lax.optimization_barrier((quarter, row_labels, row_weights))
    own, inverse_rms = norm_call(quarter, gain)

    blocks = [own, to_colour(own, 3), to_colour(own, 2), to_colour(own, 1)]
    first_mate = other_core(own)
    early = logits_call(tint, head, (0,), blocks[:1])
    blocks[1], blocks[2], blocks[3], early = lax.optimization_barrier((*blocks[1:], early))
    mates = [first_mate] + [other_core(b) for b in blocks[1:]]
    theirs = logits_call(tint, head, (0,), mates[:1])
    ours = logits_call(tint, head, (1, 2, 3), blocks[1:])
    logits, lse = last_call(tint, head, mates[1:], early, ours, theirs)
    parts = lax.all_to_all(lse, AXES, 0, 0, tiled=True)
    near = fetch(head, lse)
    parts, near = lax.optimization_barrier((parts, near))
    turned, dlogits = dlogits_call(jnp.stack([device, core]), logits, parts, row_labels, row_weights)

    halves = [back_call(tint, dlogits, near, away) for away in (1, 2, 3)]
    sums = [(ours + other_core(theirs).astype(F32)).astype(BF16) for ours, theirs in halves]
    arrived = [to_colour(s, away) for s, away in zip(sums, (1, 2, 3))]
    late, _ = lax.optimization_barrier((dlogits, sums[2]))
    ours, theirs = back_call(tint, late, near, 0)
    quarter = ours + other_core(theirs).astype(F32) + sum(a.astype(F32) for a in arrived)
    terms = lax.all_to_all(quarter.astype(BF16).reshape(64, 16, 512), CHIPS, 0, 0, tiled=True)
    head_grad = head_call(tint, turned, blocks, mates)
    terms, head_grad = lax.optimization_barrier((terms, head_grad))

    place = (y * 2 + zl) * 2 + zh
    inverse_here = lax.dynamic_slice_in_dim(inverse_rms, place * 16, 16, 0)
    gated, unit, inner, gain_part = tail_call(terms, rows, inverse_here, norm_gain.reshape(1, 2048))
    inners = [inner] + [move(inner, lambda y, z, c, x, k=k: (y, z, c, x + k)) for k in (1, 2, 3)]
    gain_other = move(gain_part, lambda y, z, c, x: (y, z + 2, c, x))
    placed = exit_call(chosen, gated, unit, inverse_here, *inners, gain_part, gain_other)
    came = lax.all_to_all(placed, PIPE, 0, 0, tiled=True)
    gain_grad = jnp.sum(came[:, :, 2048:].astype(F32).reshape(16, 8, 2, 256), axis=(0, 2)).reshape(2048)
    from_next = move(section_cotangent, back_one)
    residual_grad = (came[:, :, :2048].reshape(1, 128, 2048).astype(F32) + from_next.astype(F32)).astype(BF16)
    return head_grad, residual_grad, gain_grad


def solution(mesh):
    fine = Mesh(mesh.devices.reshape(SIZES), AXES)
    in_specs = (
        P(PIPE, "zh", "x"),
        P(PIPE, "zh", "x"),
        P("x"),
        P(AXES, None),
        P("zh"),
        P("zh"),
        P(),
    )
    out_specs = (P(AXES, None), P(PIPE, "zh", "x"), P("x"))
    return jax.shard_map(local, mesh=fine, in_specs=in_specs, out_specs=out_specs, check_vma=False)
```

```python
import functools

import jax
import jax.numpy as jnp
import numpy as np
from jax import lax
from jax.experimental import pallas as pl
from jax.experimental.pallas import tpu as pltpu
from jax.sharding import Mesh, PartitionSpec as P

NORM_EPS = 1e-05
AXES = ("y", "zl", "c", "x", "zh")
SIZES = (4, 2, 2, 4, 2)
CHIPS = ("x", "y", "zl", "zh")
PIPE = ("y", "zl", "c")
F32, BF16 = jnp.float32, jnp.bfloat16
NT = (((1,), (1,)), ((), ()))
LIMIT = 16 << 20
COLOURS = [(x + 2 * y + 3 * (2 * zh + zl)) % 4 for x in range(4) for y in range(4) for zl in range(2) for zh in range(2)]


def route(step):
    pairs = []
    for source in range(128):
        y, zl, c, x, zh = (int(i) for i in np.unravel_index(source, SIZES))
        there = step(y, 2 * zh + zl, c, x)
        if there is not None:
            y, z, c, x = there[0] % 4, there[1] % 4, there[2] % 2, there[3] % 4
            pairs.append((source, int(np.ravel_multi_index((y, z % 2, c, x, z // 2), SIZES))))
    return pairs


def move(block, step):
    return lax.ppermute(block, AXES, route(step))


def other_core(block):
    return move(block, lambda y, z, c, x: (y, z, 1 - c, x))


def to_colour(block, away):
    if away == 1:
        return move(block, lambda y, z, c, x: (y, z - 1, c, x) if c else (y, z, c, x + 1))
    if away == 3:
        return move(block, lambda y, z, c, x: (y, z + 1, c, x) if c else (y, z, c, x - 1))
    return move(block, lambda y, z, c, x: (y - 1 if c else y + 1, z, c, x))


def back_one(y, z, c, x):
    section = (y * 2 + z % 2) * 2 + c - 1
    return None if section < 0 else (section // 4, z // 2 * 2 + section // 2 % 2, section % 2, x)


def call(kernel, scalars, operands, outs, flops=0, moved=1 << 20):
    vmem = pl.BlockSpec(memory_space=pltpu.VMEM)
    smem = [] if scalars is None else [pl.BlockSpec(memory_space=pltpu.SMEM)]
    held = [pltpu.with_memory_space_constraint(o, pltpu.VMEM) for o in operands]
    return pl.pallas_call(
        kernel,
        in_specs=smem + [vmem] * len(operands),
        out_specs=[vmem] * len(outs),
        out_shape=[(jax.ShapeDtypeStruct if place else pltpu.VMEM)(shape, kind) for shape, kind, *place in outs],
        cost_estimate=pl.CostEstimate(flops=flops, bytes_accessed=moved, transcendentals=0),
        compiler_params=pltpu.CompilerParams(vmem_limit_bytes=LIMIT),
    )(*([] if scalars is None else [scalars]), *held)


def columns(tint, t, away):
    return pl.ds(pl.multiple_of(t * 2048 + tint[away] * 512, 512), 512)


def slots_kernel(rows, out):
    wide = rows[...].astype(F32)
    squares = jnp.sum(wide * wide, axis=1, keepdims=True)
    high = squares.astype(BF16).astype(F32)
    middle = (squares - high).astype(BF16).astype(F32)
    low = squares - high - middle
    lane = lax.broadcasted_iota(jnp.int32, (16, 128), 1)
    extra = jnp.where(lane == 0, high, jnp.where(lane == 1, middle, jnp.where(lane == 2, low, 0.0))).astype(BF16)
    for chip, colour in enumerate(COLOURS):
        out[chip, :, :512] = rows[:, colour * 512 : (colour + 1) * 512]
        out[chip, :, 512:] = extra


def slots_call(rows):
    return call(slots_kernel, None, [rows], [((64, 16, 640), BF16, True)])[0]


def norm_kernel(came, gain, own, inverse_rms):
    for group in range(16):
        span = slice(group * 16, (group + 1) * 16)
        squares = sum(came[t * 16 + group, :, 512:].astype(F32) for t in range(4))
        inverse = lax.rsqrt(jnp.sum(squares, axis=1, keepdims=True) / 8192 + NORM_EPS)
        inverse_rms[span, :] = jnp.broadcast_to(inverse, (16, 128))
        for t in range(4):
            unit = came[t * 16 + group, :, :512].astype(F32) * inverse
            own[t, span, :] = (unit * gain[t : t + 1, :]).astype(BF16)


def norm_call(came, gain):
    return call(norm_kernel, None, [came, gain], [((4, 256, 512), BF16), ((256, 128), F32, True)], moved=2 << 20)


def near_columns(t, away):
    return away * 4 + t


def fetch_columns(head, near, sems, tint, aways):
    copies = []
    for away in aways:
        for t in range(4):
            at = near_columns(t, away)
            copies.append(pltpu.make_async_copy(head.at[:, columns(tint, t, away)], near.at[at], sems.at[at]))
            copies[-1].start()
    return copies


def early_kernel(tint, head, block, near, total, sems):
    copies = fetch_columns(head, near, sems, tint, range(4))
    for t in range(4):
        copies[t].wait()
        part = lax.dot_general(near[near_columns(t, 0)], block[t], NT, preferred_element_type=F32)
        total[...] = part if t == 0 else total[...] + part
    for copy in copies[4:]:
        copy.wait()


def early_call(tint, head, block):
    vmem = pl.BlockSpec(memory_space=pltpu.VMEM)
    return pl.pallas_call(
        early_kernel,
        in_specs=[pl.BlockSpec(memory_space=pltpu.SMEM), pl.BlockSpec(memory_space=pl.ANY), vmem],
        out_specs=[vmem] * 2,
        out_shape=[pltpu.VMEM((16, 512, 512), BF16), pltpu.VMEM((512, 256), F32)],
        scratch_shapes=[pltpu.SemaphoreType.DMA((16,))],
        cost_estimate=pl.CostEstimate(flops=2 * 512 * 256 * 2048, bytes_accessed=9 << 20, transcendentals=0),
        compiler_params=pltpu.CompilerParams(vmem_limit_bytes=LIMIT),
    )(tint, head, pltpu.with_memory_space_constraint(block, pltpu.VMEM))


def add_up(aways, near, blocks, total):
    def part(t):
        return sum(
            lax.dot_general(near[near_columns(t, away)], block[t], NT, preferred_element_type=F32)
            for away, block in zip(aways, blocks)
        )

    total[...] = part(0)

    @pl.loop(1, 4)
    def _(t):
        total[...] += part(t)


def logits_kernel(aways, near, *refs):
    add_up(aways, near, refs[:-1], refs[-1])


def logits_call(near, aways, blocks):
    flops = 2 * 512 * 256 * 2048 * len(aways)
    kernel = functools.partial(logits_kernel, aways)
    return call(kernel, None, [near, *blocks], [((512, 256), F32)], flops, len(aways) << 21)[0]


def last_kernel(core, near, block_1, block_2, block_3, early, ours, theirs, logits, lse, total):
    add_up((1, 2, 3), near, (block_1, block_2, block_3), total)
    logits[:, :256] = early[...] + ours[...]
    logits[:, 256:] = theirs[...] + total[...]
    values = logits[...]
    top = jnp.max(values, axis=0, keepdims=True)
    sums = top + jnp.log(jnp.sum(jnp.exp(values - top), axis=0, keepdims=True))
    quarters = [sums[:, i * 128 : (i + 1) * 128] for i in range(4)]
    in_order = jnp.concatenate(quarters, axis=0)
    swapped = jnp.concatenate(quarters[2:] + quarters[:2], axis=0)
    lse[...] = jnp.broadcast_to(jnp.where(core[4] == 0, in_order, swapped)[None], (128, 4, 128))


def last_call(tint, near, blocks, early, ours, theirs):
    outs = [((512, 512), F32, True), ((128, 4, 128), F32, True), ((512, 256), F32)]
    return call(last_kernel, tint, [near, *blocks, early, ours, theirs], outs, 6 * 512 * 256 * 2048, 9 << 20)[:2]


def turn_kernel(info, logits, head, parts, labels, weights, turned, dlogits, inner, near, own, other, held, sems):
    first = pltpu.make_async_copy(logits, held, sems.at[16])
    first.start()
    copies = fetch_columns(head, near, sems, info, (1, 2, 3, 0))
    lse = parts[...]
    top = jnp.max(lse, axis=0)
    log_total = top + jnp.log(jnp.sum(jnp.exp(lse - top[None]), axis=0))
    quarters = [log_total[i : i + 1] for i in range(4)]
    in_order = jnp.concatenate(quarters, axis=1)
    swapped = jnp.concatenate(quarters[2:] + quarters[:2], axis=1)
    log_total = jnp.where(info[4] == 0, in_order, swapped)
    first.wait()
    probs = jnp.exp(held[...] - log_total)
    ids = info[5] * 512 + lax.broadcasted_iota(jnp.int32, (512, 512), 0)
    hot = jnp.where(ids == labels[...], 1.0, 0.0)
    values = (weights[...] * (probs - hot)).astype(BF16)
    turned[...] = values
    dlogits[...] = values.T
    inner[...] = jnp.sum(values.astype(F32) * held[...], axis=0, keepdims=True)
    for t in range(4):
        copies[t].wait()
        value = jnp.dot(dlogits[...], near[near_columns(t, 1)], preferred_element_type=F32)
        own[t] = value[:256]
        other[t] = value[256:].astype(BF16)
    for copy in copies[4:]:
        copy.wait()


def turn_call(info, logits, head, parts, labels, weights):
    vmem, anywhere = pl.BlockSpec(memory_space=pltpu.VMEM), pl.BlockSpec(memory_space=pl.ANY)
    return pl.pallas_call(
        turn_kernel,
        in_specs=[pl.BlockSpec(memory_space=pltpu.SMEM), anywhere, anywhere, vmem, vmem, vmem],
        out_specs=[vmem] * 6,
        out_shape=[
            jax.ShapeDtypeStruct((512, 512), BF16),
            pltpu.VMEM((512, 512), BF16),
            jax.ShapeDtypeStruct((1, 512), F32),
            pltpu.VMEM((16, 512, 512), BF16),
            pltpu.VMEM((4, 256, 512), F32),
            pltpu.VMEM((4, 256, 512), BF16),
        ],
        scratch_shapes=[pltpu.VMEM((512, 512), F32), pltpu.SemaphoreType.DMA((17,))],
        cost_estimate=pl.CostEstimate(flops=2 * 512 * 512 * 2048, bytes_accessed=9 << 20, transcendentals=0),
        compiler_params=pltpu.CompilerParams(vmem_limit_bytes=LIMIT),
    )(info, logits, head, parts, labels, weights)


def back_kernel(away, dlogits, near, own, other):
    @pl.loop(0, 4)
    def _(t):
        value = jnp.dot(dlogits[...], near[near_columns(t, away)], preferred_element_type=F32)
        own[t] = value[:256]
        other[t] = value[256:].astype(BF16)


def back_call(dlogits, near, away):
    kernel = functools.partial(back_kernel, away)
    outs = [((4, 256, 512), F32), ((4, 256, 512), BF16)]
    return call(kernel, None, [dlogits, near], outs, 2 * 512 * 512 * 2048, 4 << 20)


def head_kernel(tint, turned, *refs):
    out = refs[-1]
    for away in range(4):
        own, other = refs[away], refs[4 + away]
        value = jnp.dot(turned[:, :256], own[0], preferred_element_type=F32)
        value += jnp.dot(turned[:, 256:], other[0], preferred_element_type=F32)
        out[:, pl.ds(pl.multiple_of(tint[away] * 512, 512), 512)] = value.astype(BF16)


def head_call(tint, turned, own, other):
    block = pl.BlockSpec((1, 256, 512), lambda t, tint: (t, 0, 0))
    return pl.pallas_call(
        head_kernel,
        grid_spec=pltpu.PrefetchScalarGridSpec(
            num_scalar_prefetch=1,
            grid=(4,),
            in_specs=[pl.BlockSpec((512, 512), lambda t, tint: (0, 0))] + [block] * 8,
            out_specs=pl.BlockSpec((512, 2048), lambda t, tint: (0, t)),
        ),
        out_shape=jax.ShapeDtypeStruct((512, 8192), BF16),
        cost_estimate=pl.CostEstimate(flops=2 * 512 * 512 * 8192, bytes_accessed=17 << 20, transcendentals=0),
        compiler_params=pltpu.CompilerParams(vmem_limit_bytes=LIMIT),
    )(tint, turned, *own, *other)


def three_parts(value):
    high = value.astype(BF16).astype(F32)
    middle = (value - high).astype(BF16).astype(F32)
    return high, middle, value - high - middle


def join_kernel(came, inverse_rms, ours, swapped, one, two, three, inner, out):
    products = [part[i : i + 1] for part in three_parts(inner[...]) for i in range(2)]
    for t in range(4):
        gain = jnp.zeros((1, 512), F32)
        for group in range(16):
            span = slice(group * 16, (group + 1) * 16)
            total = ours[t, span] + swapped[t, span].astype(F32)
            total += one[t, span].astype(F32) + two[t, span].astype(F32) + three[t, span].astype(F32)
            out[t * 16 + group, :, :512] = total.astype(BF16)
            unit = came[t * 16 + group, :, :512].astype(F32) * inverse_rms[span, :1]
            gain += jnp.sum(total * unit, axis=0, keepdims=True)
        parts = [part[:, i * 128 : (i + 1) * 128] for part in three_parts(gain)[:2] for i in range(4)]
        extra = jnp.concatenate(parts + products + [jnp.zeros((2, 128), F32)], axis=0).astype(BF16)
        for group in range(16):
            out[t * 16 + group, :, 512:] = extra


def join_call(*operands):
    return call(join_kernel, None, operands, [((64, 16, 640), BF16, True)], moved=6 << 20)[0]


def tail_kernel(info, terms, rows, inverse_rms, gain, placed, gain_grad):
    sums = [None] * 4
    for chip, colour in enumerate(COLOURS):
        term = terms[chip].astype(F32)
        sums[colour] = term if sums[colour] is None else sums[colour] + term
    products = sum(s[8:14, 512:] for s in sums)
    lane = lax.broadcasted_iota(jnp.int32, (16, 128), 1)
    row = info[2] * 16 + lax.broadcasted_iota(jnp.int32, (16, 128), 0)
    here = [jnp.where(lane + 128 * (i % 2) == row, products[i : i + 1], 0.0) for i in range(6)]
    inner = jnp.sum(sum(here), axis=1, keepdims=True) / 8192
    inverse = inverse_rms[:, :1]
    for colour, total in enumerate(sums):
        span = slice(colour * 512, (colour + 1) * 512)
        gain_grad[colour * 4 : (colour + 1) * 4, :] = total[:4, 512:] + total[4:8, 512:]
        unit = rows[:, span].astype(F32) * inverse
        exit_grad = inverse * (total[:, :512] * gain[:, span] - unit * inner)
        for section in range(16):
            value = jnp.where(info[0] == section, exit_grad[:8], jnp.where(info[1] == section, exit_grad[8:], 0.0))
            placed[section, :, span] = value.astype(BF16)


def tail_call(info, *operands):
    outs = [((16, 8, 2048), BF16, True), ((16, 128), F32)]
    return call(tail_kernel, info, operands, outs, moved=2 << 20)


def local(hidden, section_cotangent, norm_gain, head, labels, loss_mask, exit_on):
    core, x, y, zl, zh = (lax.axis_index(a) for a in ("c", "x", "y", "zl", "zh"))
    device = lax.axis_index(AXES).astype(jnp.int32)
    colour = (x + 2 * y + 3 * (2 * zh + zl)) % 4
    aways = (colour + jnp.arange(4, dtype=jnp.int32)) % 4
    tint = jnp.concatenate([aways, core.reshape(1), device.reshape(1)]).astype(jnp.int32)

    came = lax.all_to_all(hidden.reshape(16, 8, 2048), PIPE, 0, 0, tiled=True)
    section_ids = jnp.arange(16, dtype=jnp.int32)
    first = jnp.min(jnp.where(exit_on == 1, section_ids, 16))
    second = jnp.max(jnp.where(exit_on == 1, section_ids, -1))
    chosen = jnp.stack([first, second])
    scores = (chosen + 1).astype(F32)
    weights = scores / jnp.sum(scores)

    turns = [norm_gain] + [move(norm_gain, lambda y, z, c, x, k=k: (y, z, c, x + k)) for k in (1, 2, 3)]
    ring = jnp.stack(turns[::-1] * 2)
    gain = lax.dynamic_slice(ring, ((3 - x) % 4, colour * 512), (4, 512))
    came, gain = lax.optimization_barrier((came, gain))
    rows = jnp.concatenate([lax.dynamic_index_in_dim(came, s, 0, False) for s in (first, second)])
    token_info = jnp.stack([labels, loss_mask])
    other_info = move(token_info, lambda y, z, c, x: (y, z + 2, c, x))
    both = jnp.where(zh == 0, jnp.stack([token_info, other_info]), jnp.stack([other_info, token_info]))
    by_row = jnp.broadcast_to(
        both.reshape(2, 2, 4, 2, 2, 8).transpose(4, 1, 2, 3, 0, 5)[:, :, :, :, :, None], (2, 2, 4, 2, 2, 2, 8)
    )
    by_row = jnp.where(core == 0, by_row, by_row[::-1])
    row_labels = by_row[:, 0].reshape(1, 512)
    row_weights = (weights[:, None] * by_row[:, 1].astype(F32)).reshape(1, 512)

    quarter = lax.all_to_all(slots_call(rows), CHIPS, 0, 0, tiled=True)
    quarter, row_labels, row_weights = lax.optimization_barrier((quarter, row_labels, row_weights))
    own, inverse_rms = norm_call(quarter, gain)

    blocks = [own, to_colour(own, 3), to_colour(own, 2), to_colour(own, 1)]
    first_mate = other_core(own)
    near, early = early_call(tint, head, own)
    theirs = logits_call(near, (0,), [first_mate])
    blocks[1], blocks[2], blocks[3], early, theirs = lax.optimization_barrier((*blocks[1:], early, theirs))
    mates = [first_mate] + [other_core(b) for b in blocks[1:]]
    ours = logits_call(near, (1, 2, 3), blocks[1:])
    logits, lse = last_call(tint, near, mates[1:], early, ours, theirs)
    parts = lax.all_to_all(lse, AXES, 0, 0, tiled=True)
    turned, dlogits, inner, near, *first_half = turn_call(tint, logits, head, parts, row_labels, row_weights)

    halves = [first_half] + [back_call(dlogits, near, away) for away in (2, 3)]
    sums = [(ours + other_core(theirs).astype(F32)).astype(BF16) for ours, theirs in halves]
    arrived = [to_colour(s, away) for s, away in zip(sums, (1, 2, 3))]
    late, inner, _ = lax.optimization_barrier((dlogits, inner, sums[2]))
    ours, theirs = back_call(late, near, 0)
    inner = inner.reshape(2, 2, 128)
    inner = inner[0] + other_core(inner[1])
    slots = join_call(quarter, inverse_rms, ours, other_core(theirs), *arrived, inner)
    terms = lax.all_to_all(slots, CHIPS, 0, 0, tiled=True)
    head_grad = head_call(tint, turned, blocks, mates)
    place = (y * 2 + zl) * 2 + zh
    inverse_here = lax.dynamic_slice_in_dim(inverse_rms, place * 16, 16, 0)
    terms, head_grad, inverse_here = lax.optimization_barrier((terms, head_grad, inverse_here))
    info = jnp.concatenate([chosen, place.reshape(1)]).astype(jnp.int32)
    placed, gain_grad = tail_call(info, terms, rows, inverse_here, norm_gain.reshape(1, 2048))
    came = lax.all_to_all(placed, PIPE, 0, 0, tiled=True)
    gain_grad = (gain_grad + other_core(gain_grad)).reshape(2048)
    from_next = move(section_cotangent, back_one)
    residual_grad = (came.reshape(1, 128, 2048).astype(F32) + from_next.astype(F32)).astype(BF16)
    return head_grad, residual_grad, gain_grad


def solution(mesh):
    fine = Mesh(mesh.devices.reshape(SIZES), AXES)
    in_specs = (
        P(PIPE, "zh", "x"),
        P(PIPE, "zh", "x"),
        P("x"),
        P(AXES, None),
        P("zh"),
        P("zh"),
        P(),
    )
    out_specs = (P(AXES, None), P(PIPE, "zh", "x"), P("x"))
    return jax.shard_map(local, mesh=fine, in_specs=in_specs, out_specs=out_specs, check_vma=False)
```

```python
import functools

import jax
import jax.numpy as jnp
import numpy as np
from jax import lax
from jax.experimental import pallas as pl
from jax.experimental.pallas import tpu as pltpu
from jax.sharding import Mesh, PartitionSpec as P

NORM_EPS = 1e-05
AXES = ("y", "zl", "c", "x", "zh")
SIZES = (4, 2, 2, 4, 2)
CHIPS = ("x", "y", "zl", "zh")
PIPE = ("y", "zl", "c")
F32, BF16 = jnp.float32, jnp.bfloat16
NT = (((1,), (1,)), ((), ()))
LIMIT = 16 << 20
COLOURS = [(x + 2 * y + 3 * (2 * zh + zl)) % 4 for x in range(4) for y in range(4) for zl in range(2) for zh in range(2)]


def route(step):
    pairs = []
    for source in range(128):
        y, zl, c, x, zh = (int(i) for i in np.unravel_index(source, SIZES))
        there = step(y, 2 * zh + zl, c, x)
        if there is not None:
            y, z, c, x = there[0] % 4, there[1] % 4, there[2] % 2, there[3] % 4
            pairs.append((source, int(np.ravel_multi_index((y, z % 2, c, x, z // 2), SIZES))))
    return pairs


def move(block, step):
    return lax.ppermute(block, AXES, route(step))


def other_core(block):
    return move(block, lambda y, z, c, x: (y, z, 1 - c, x))


def to_colour(block, away):
    if away == 1:
        return move(block, lambda y, z, c, x: (y, z - 1, c, x) if c else (y, z, c, x + 1))
    if away == 3:
        return move(block, lambda y, z, c, x: (y, z + 1, c, x) if c else (y, z, c, x - 1))
    return move(block, lambda y, z, c, x: (y - 1 if c else y + 1, z, c, x))


def back_one(y, z, c, x):
    section = (y * 2 + z % 2) * 2 + c - 1
    return None if section < 0 else (section // 4, z // 2 * 2 + section // 2 % 2, section % 2, x)


def call(kernel, scalars, operands, outs, flops=0, moved=1 << 20):
    vmem = pl.BlockSpec(memory_space=pltpu.VMEM)
    smem = [] if scalars is None else [pl.BlockSpec(memory_space=pltpu.SMEM)]
    held = [pltpu.with_memory_space_constraint(o, pltpu.VMEM) for o in operands]
    return pl.pallas_call(
        kernel,
        in_specs=smem + [vmem] * len(operands),
        out_specs=[vmem] * len(outs),
        out_shape=[(jax.ShapeDtypeStruct if place else pltpu.VMEM)(shape, kind) for shape, kind, *place in outs],
        cost_estimate=pl.CostEstimate(flops=flops, bytes_accessed=moved, transcendentals=0),
        compiler_params=pltpu.CompilerParams(vmem_limit_bytes=LIMIT),
    )(*([] if scalars is None else [scalars]), *held)


def columns(tint, t, away):
    return pl.ds(pl.multiple_of(t * 2048 + tint[away] * 512, 512), 512)


def diagonal():
    return lax.broadcasted_iota(jnp.int32, (16, 128), 0) == lax.broadcasted_iota(jnp.int32, (16, 128), 1)


def slots_kernel(rows, out):
    wide = rows[...].astype(F32)
    squares = jnp.sum(wide * wide, axis=1, keepdims=True)
    along = jnp.sum(jnp.where(diagonal(), squares, 0.0), axis=0, keepdims=True)
    extra = jnp.concatenate([*three_parts(along), jnp.zeros((5, 128), F32)], axis=0).astype(BF16)
    for chip, colour in enumerate(COLOURS):
        for i in range(4):
            start = colour * 512 + i * 128
            out[chip, i * 16 : (i + 1) * 16, :] = rows[:, start : start + 128]
        out[chip, 64:, :] = extra


def slots_call(rows):
    return call(slots_kernel, None, [rows], [((64, 72, 128), BF16, True)])[0]


def inverse_of(came, group):
    squares = sum(came[t * 16 + group, 64:, :].astype(F32) for t in range(4))
    along = jnp.sum(squares, axis=0, keepdims=True)
    squares = jnp.sum(jnp.where(diagonal(), along, 0.0), axis=1, keepdims=True)
    return lax.rsqrt(squares / 8192 + NORM_EPS)


def norm_kernel(came, gain, own):
    for group in range(16):
        span = slice(group * 16, (group + 1) * 16)
        inverse = inverse_of(came, group)
        for t in range(4):
            for i in range(4):
                unit = came[t * 16 + group, i * 16 : (i + 1) * 16, :].astype(F32) * inverse
                lanes = slice(i * 128, (i + 1) * 128)
                own[t, span, lanes] = (unit * gain[t : t + 1, lanes]).astype(BF16)


def norm_call(came, gain):
    return call(norm_kernel, None, [came, gain], [((4, 256, 512), BF16)], moved=2 << 20)[0]


def near_columns(t, away):
    return away * 4 + t


def fetch_columns(head, near, sems, tint, aways):
    copies = []
    for away in aways:
        for t in range(4):
            at = near_columns(t, away)
            copies.append(pltpu.make_async_copy(head.at[:, columns(tint, t, away)], near.at[at], sems.at[at]))
            copies[-1].start()
    return copies


def early_kernel(tint, head, block, near, total, sems):
    copies = fetch_columns(head, near, sems, tint, range(4))
    for t in range(4):
        copies[t].wait()
        part = lax.dot_general(near[near_columns(t, 0)], block[t], NT, preferred_element_type=F32)
        total[...] = part if t == 0 else total[...] + part
    for copy in copies[4:]:
        copy.wait()


def early_call(tint, head, block):
    vmem = pl.BlockSpec(memory_space=pltpu.VMEM)
    return pl.pallas_call(
        early_kernel,
        in_specs=[pl.BlockSpec(memory_space=pltpu.SMEM), pl.BlockSpec(memory_space=pl.ANY), vmem],
        out_specs=[vmem] * 2,
        out_shape=[pltpu.VMEM((16, 512, 512), BF16), pltpu.VMEM((512, 256), F32)],
        scratch_shapes=[pltpu.SemaphoreType.DMA((16,))],
        cost_estimate=pl.CostEstimate(flops=2 * 512 * 256 * 2048, bytes_accessed=9 << 20, transcendentals=0),
        compiler_params=pltpu.CompilerParams(vmem_limit_bytes=LIMIT),
    )(tint, head, pltpu.with_memory_space_constraint(block, pltpu.VMEM))


def add_up(aways, near, blocks, total):
    def part(t):
        return sum(
            lax.dot_general(near[near_columns(t, away)], block[t], NT, preferred_element_type=F32)
            for away, block in zip(aways, blocks)
        )

    total[...] = part(0)

    @pl.loop(1, 4)
    def _(t):
        total[...] += part(t)


def logits_kernel(aways, near, *refs):
    add_up(aways, near, refs[:-1], refs[-1])


def logits_call(near, aways, blocks):
    flops = 2 * 512 * 256 * 2048 * len(aways)
    kernel = functools.partial(logits_kernel, aways)
    return call(kernel, None, [near, *blocks], [((512, 256), F32)], flops, len(aways) << 21)[0]


def last_kernel(core, near, block_1, block_2, block_3, early, ours, theirs, logits, lse, total):
    add_up((1, 2, 3), near, (block_1, block_2, block_3), total)
    logits[:, :256] = early[...] + ours[...]
    logits[:, 256:] = theirs[...] + total[...]
    values = logits[...]
    top = jnp.max(values, axis=0, keepdims=True)
    sums = top + jnp.log(jnp.sum(jnp.exp(values - top), axis=0, keepdims=True))
    quarters = [sums[:, i * 128 : (i + 1) * 128] for i in range(4)]
    in_order = jnp.concatenate(quarters, axis=0)
    swapped = jnp.concatenate(quarters[2:] + quarters[:2], axis=0)
    lse[...] = jnp.broadcast_to(jnp.where(core[4] == 0, in_order, swapped)[None], (128, 4, 128))


def last_call(tint, near, blocks, early, ours, theirs):
    outs = [((512, 512), F32, True), ((128, 4, 128), F32, True), ((512, 256), F32)]
    return call(last_kernel, tint, [near, *blocks, early, ours, theirs], outs, 6 * 512 * 256 * 2048, 9 << 20)[:2]


def turn_kernel(info, logits, head, parts, labels, weights, turned, dlogits, inner, near, own, other, held, sems):
    first = pltpu.make_async_copy(logits, held, sems.at[16])
    first.start()
    copies = fetch_columns(head, near, sems, info, (1, 2, 3, 0))
    lse = parts[...]
    top = jnp.max(lse, axis=0)
    log_total = top + jnp.log(jnp.sum(jnp.exp(lse - top[None]), axis=0))
    quarters = [log_total[i : i + 1] for i in range(4)]
    in_order = jnp.concatenate(quarters, axis=1)
    swapped = jnp.concatenate(quarters[2:] + quarters[:2], axis=1)
    log_total = jnp.where(info[4] == 0, in_order, swapped)
    first.wait()
    probs = jnp.exp(held[...] - log_total)
    ids = info[5] * 512 + lax.broadcasted_iota(jnp.int32, (512, 512), 0)
    hot = jnp.where(ids == labels[...], 1.0, 0.0)
    values = (weights[...] * (probs - hot)).astype(BF16)
    turned[...] = values
    dlogits[...] = values.T
    inner[...] = jnp.sum(values.astype(F32) * held[...], axis=0, keepdims=True)
    for t in range(4):
        copies[t].wait()
        value = jnp.dot(dlogits[...], near[near_columns(t, 1)], preferred_element_type=F32)
        own[t] = value[:256]
        other[t] = value[256:].astype(BF16)
    for copy in copies[4:]:
        copy.wait()


def turn_call(info, logits, head, parts, labels, weights):
    vmem, anywhere = pl.BlockSpec(memory_space=pltpu.VMEM), pl.BlockSpec(memory_space=pl.ANY)
    return pl.pallas_call(
        turn_kernel,
        in_specs=[pl.BlockSpec(memory_space=pltpu.SMEM), anywhere, anywhere, vmem, vmem, vmem],
        out_specs=[vmem] * 6,
        out_shape=[
            jax.ShapeDtypeStruct((512, 512), BF16),
            pltpu.VMEM((512, 512), BF16),
            jax.ShapeDtypeStruct((1, 512), F32),
            pltpu.VMEM((16, 512, 512), BF16),
            pltpu.VMEM((4, 256, 512), F32),
            pltpu.VMEM((4, 256, 512), BF16),
        ],
        scratch_shapes=[pltpu.VMEM((512, 512), F32), pltpu.SemaphoreType.DMA((17,))],
        cost_estimate=pl.CostEstimate(flops=2 * 512 * 512 * 2048, bytes_accessed=9 << 20, transcendentals=0),
        compiler_params=pltpu.CompilerParams(vmem_limit_bytes=LIMIT),
    )(info, logits, head, parts, labels, weights)


def back_kernel(away, dlogits, near, own, other):
    @pl.loop(0, 4)
    def _(t):
        value = jnp.dot(dlogits[...], near[near_columns(t, away)], preferred_element_type=F32)
        own[t] = value[:256]
        other[t] = value[256:].astype(BF16)


def back_call(dlogits, near, away):
    kernel = functools.partial(back_kernel, away)
    outs = [((4, 256, 512), F32), ((4, 256, 512), BF16)]
    return call(kernel, None, [dlogits, near], outs, 2 * 512 * 512 * 2048, 4 << 20)


def head_kernel(tint, turned, *refs):
    out = refs[-1]
    for away in range(4):
        own, other = refs[away], refs[4 + away]
        value = jnp.dot(turned[:, :256], own[0], preferred_element_type=F32)
        value += jnp.dot(turned[:, 256:], other[0], preferred_element_type=F32)
        out[:, pl.ds(pl.multiple_of(tint[away] * 512, 512), 512)] = value.astype(BF16)


def head_call(tint, turned, own, other):
    block = pl.BlockSpec((1, 256, 512), lambda t, tint: (t, 0, 0))
    return pl.pallas_call(
        head_kernel,
        grid_spec=pltpu.PrefetchScalarGridSpec(
            num_scalar_prefetch=1,
            grid=(4,),
            in_specs=[pl.BlockSpec((512, 512), lambda t, tint: (0, 0))] + [block] * 8,
            out_specs=pl.BlockSpec((512, 2048), lambda t, tint: (0, t)),
        ),
        out_shape=jax.ShapeDtypeStruct((512, 8192), BF16),
        cost_estimate=pl.CostEstimate(flops=2 * 512 * 512 * 8192, bytes_accessed=17 << 20, transcendentals=0),
        compiler_params=pltpu.CompilerParams(vmem_limit_bytes=LIMIT),
    )(tint, turned, *own, *other)


def three_parts(value):
    high = value.astype(BF16).astype(F32)
    middle = (value - high).astype(BF16).astype(F32)
    return high, middle, value - high - middle


def join_kernel(came, ours, swapped, one, two, three, inner, out, inverse_rms):
    for group in range(16):
        inverse_rms[group * 16 : (group + 1) * 16, :] = jnp.broadcast_to(inverse_of(came, group), (16, 128))
    products = [part[i : i + 1] for part in three_parts(inner[...]) for i in range(2)]
    for t in range(4):
        gain = jnp.zeros((1, 512), F32)
        for group in range(16):
            span = slice(group * 16, (group + 1) * 16)
            total = ours[t, span] + swapped[t, span].astype(F32)
            total += one[t, span].astype(F32) + two[t, span].astype(F32) + three[t, span].astype(F32)
            out[t * 16 + group, :, :512] = total.astype(BF16)
            pieces = [came[t * 16 + group, i * 16 : (i + 1) * 16, :] for i in range(4)]
            unit = jnp.concatenate(pieces, axis=1).astype(F32) * inverse_rms[span, :1]
            gain += jnp.sum(total * unit, axis=0, keepdims=True)
        parts = [part[:, i * 128 : (i + 1) * 128] for part in three_parts(gain)[:2] for i in range(4)]
        extra = jnp.concatenate(parts + products + [jnp.zeros((2, 128), F32)], axis=0).astype(BF16)
        for group in range(16):
            out[t * 16 + group, :, 512:] = extra


def join_call(*operands):
    outs = [((64, 16, 640), BF16, True), ((256, 128), F32)]
    return call(join_kernel, None, operands, outs, moved=6 << 20)


def tail_kernel(info, terms, rows, inverse_rms, gain, placed, gain_grad):
    sums = [None] * 4
    for chip, colour in enumerate(COLOURS):
        term = terms[chip].astype(F32)
        sums[colour] = term if sums[colour] is None else sums[colour] + term
    products = sum(s[8:14, 512:] for s in sums)
    lane = lax.broadcasted_iota(jnp.int32, (16, 128), 1)
    row = info[2] * 16 + lax.broadcasted_iota(jnp.int32, (16, 128), 0)
    here = [jnp.where(lane + 128 * (i % 2) == row, products[i : i + 1], 0.0) for i in range(6)]
    inner = jnp.sum(sum(here), axis=1, keepdims=True) / 8192
    inverse = inverse_rms[:, :1]
    for colour, total in enumerate(sums):
        span = slice(colour * 512, (colour + 1) * 512)
        gain_grad[colour * 4 : (colour + 1) * 4, :] = total[:4, 512:] + total[4:8, 512:]
        unit = rows[:, span].astype(F32) * inverse
        exit_grad = inverse * (total[:, :512] * gain[:, span] - unit * inner)
        for section in range(16):
            value = jnp.where(info[0] == section, exit_grad[:8], jnp.where(info[1] == section, exit_grad[8:], 0.0))
            placed[section, :, span] = value.astype(BF16)


def tail_call(info, *operands):
    outs = [((16, 8, 2048), BF16, True), ((16, 128), F32)]
    return call(tail_kernel, info, operands, outs, moved=2 << 20)


def hold_kernel(source, out):
    out[...] = source[...]


def add_kernel(exits, from_next, out):
    out[...] = (exits[...].astype(F32) + from_next[...].astype(F32)).astype(BF16)


def local(hidden, section_cotangent, norm_gain, head, labels, loss_mask, exit_on):
    core, x, y, zl, zh = (lax.axis_index(a) for a in ("c", "x", "y", "zl", "zh"))
    device = lax.axis_index(AXES).astype(jnp.int32)
    colour = (x + 2 * y + 3 * (2 * zh + zl)) % 4
    aways = (colour + jnp.arange(4, dtype=jnp.int32)) % 4
    tint = jnp.concatenate([aways, core.reshape(1), device.reshape(1)]).astype(jnp.int32)

    came = lax.all_to_all(hidden.reshape(16, 8, 2048), PIPE, 0, 0, tiled=True)
    section_ids = jnp.arange(16, dtype=jnp.int32)
    first = jnp.min(jnp.where(exit_on == 1, section_ids, 16))
    second = jnp.max(jnp.where(exit_on == 1, section_ids, -1))
    chosen = jnp.stack([first, second])
    scores = (chosen + 1).astype(F32)
    weights = scores / jnp.sum(scores)

    turns = [norm_gain] + [move(norm_gain, lambda y, z, c, x, k=k: (y, z, c, x + k)) for k in (1, 2, 3)]
    ring = jnp.stack(turns[::-1] * 2)
    gain = lax.dynamic_slice(ring, ((3 - x) % 4, colour * 512), (4, 512))
    came, gain = lax.optimization_barrier((came, gain))
    rows = jnp.concatenate([lax.dynamic_index_in_dim(came, s, 0, False) for s in (first, second)])
    token_info = jnp.stack([labels, loss_mask])
    other_info = move(token_info, lambda y, z, c, x: (y, z + 2, c, x))
    both = jnp.where(zh == 0, jnp.stack([token_info, other_info]), jnp.stack([other_info, token_info]))
    by_row = jnp.broadcast_to(
        both.reshape(2, 2, 4, 2, 2, 8).transpose(4, 1, 2, 3, 0, 5)[:, :, :, :, :, None], (2, 2, 4, 2, 2, 2, 8)
    )
    by_row = jnp.where(core == 0, by_row, by_row[::-1])
    row_labels = by_row[:, 0].reshape(1, 512)
    row_weights = (weights[:, None] * by_row[:, 1].astype(F32)).reshape(1, 512)

    quarter = lax.all_to_all(slots_call(rows), CHIPS, 0, 0, tiled=True)
    quarter, row_labels, row_weights = lax.optimization_barrier((quarter, row_labels, row_weights))
    own = norm_call(quarter, gain)

    blocks = [own, to_colour(own, 3), to_colour(own, 2), to_colour(own, 1)]
    first_mate = other_core(own)
    near, early = early_call(tint, head, own)
    theirs = logits_call(near, (0,), [first_mate])
    blocks[1], blocks[2], blocks[3], early, theirs = lax.optimization_barrier((*blocks[1:], early, theirs))
    mates = [first_mate] + [other_core(b) for b in blocks[1:]]
    ours = logits_call(near, (1, 2, 3), blocks[1:])
    logits, lse = last_call(tint, near, mates[1:], early, ours, theirs)
    parts = lax.all_to_all(lse, AXES, 0, 0, tiled=True)
    turned, dlogits, inner, near, *first_half = turn_call(tint, logits, head, parts, row_labels, row_weights)

    halves = [first_half] + [back_call(dlogits, near, away) for away in (2, 3)]
    sums = [(ours + other_core(theirs).astype(F32)).astype(BF16) for ours, theirs in halves]
    arrived = [to_colour(s, away) for s, away in zip(sums, (1, 2, 3))]
    inner, _ = lax.optimization_barrier((inner, sums[2]))
    inner = inner.reshape(2, 2, 128)
    inner = inner[0] + other_core(inner[1])
    late, inner = lax.optimization_barrier((dlogits, inner))
    ours, theirs = back_call(late, near, 0)
    slots, inverse_rms = join_call(quarter, ours, other_core(theirs), *arrived, inner)
    terms = lax.all_to_all(slots, CHIPS, 0, 0, tiled=True)
    head_grad = head_call(tint, turned, blocks, mates)
    place = (y * 2 + zl) * 2 + zh
    inverse_here = lax.dynamic_slice_in_dim(inverse_rms, place * 16, 16, 0)
    terms, head_grad, inverse_here = lax.optimization_barrier((terms, head_grad, inverse_here))
    info = jnp.concatenate([chosen, place.reshape(1)]).astype(jnp.int32)
    placed, gain_grad = tail_call(info, terms, rows, inverse_here, norm_gain.reshape(1, 2048))
    came = lax.all_to_all(placed, PIPE, 0, 0, tiled=True)
    gain_grad = (gain_grad + other_core(gain_grad)).reshape(2048)
    from_next = move(section_cotangent, back_one)
    from_next = call(hold_kernel, None, [from_next[0]], [((128, 2048), BF16)])[0]
    residual_grad = call(add_kernel, None, [came.reshape(128, 2048), from_next], [((128, 2048), BF16, True)])[0][None]
    return head_grad, residual_grad, gain_grad


def solution(mesh):
    fine = Mesh(mesh.devices.reshape(SIZES), AXES)
    in_specs = (
        P(PIPE, "zh", "x"),
        P(PIPE, "zh", "x"),
        P("x"),
        P(AXES, None),
        P("zh"),
        P("zh"),
        P(),
    )
    out_specs = (P(AXES, None), P(PIPE, "zh", "x"), P("x"))
    return jax.shard_map(local, mesh=fine, in_specs=in_specs, out_specs=out_specs, check_vma=False)
```

```python
import functools

import jax
import jax.numpy as jnp
import numpy as np
from jax import lax
from jax.experimental import pallas as pl
from jax.experimental.pallas import tpu as pltpu
from jax.sharding import Mesh, PartitionSpec as P

NORM_EPS = 1e-05
AXES = ("y", "zl", "c", "x", "zh")
SIZES = (4, 2, 2, 4, 2)
CHIPS = ("x", "y", "zl", "zh")
PIPE = ("y", "zl", "c")
F32, BF16 = jnp.float32, jnp.bfloat16
NT = (((1,), (1,)), ((), ()))
LIMIT = 16 << 20
COLOURS = [(x + 2 * y + 3 * (2 * zh + zl)) % 4 for x in range(4) for y in range(4) for zl in range(2) for zh in range(2)]


def route(step):
    pairs = []
    for source in range(128):
        y, zl, c, x, zh = (int(i) for i in np.unravel_index(source, SIZES))
        there = step(y, 2 * zh + zl, c, x)
        if there is not None:
            y, z, c, x = there[0] % 4, there[1] % 4, there[2] % 2, there[3] % 4
            pairs.append((source, int(np.ravel_multi_index((y, z % 2, c, x, z // 2), SIZES))))
    return pairs


def move(block, step):
    return lax.ppermute(block, AXES, route(step))


def other_core(block):
    return move(block, lambda y, z, c, x: (y, z, 1 - c, x))


def to_colour(block, away):
    if away == 1:
        return move(block, lambda y, z, c, x: (y, z - 1, c, x) if c else (y, z, c, x + 1))
    if away == 3:
        return move(block, lambda y, z, c, x: (y, z + 1, c, x) if c else (y, z, c, x - 1))
    return move(block, lambda y, z, c, x: (y - 1 if c else y + 1, z, c, x))


def back_one(y, z, c, x):
    section = (y * 2 + z % 2) * 2 + c - 1
    return None if section < 0 else (section // 4, z // 2 * 2 + section // 2 % 2, section % 2, x)


def call(kernel, scalars, operands, outs, flops=0, moved=1 << 20):
    vmem = pl.BlockSpec(memory_space=pltpu.VMEM)
    smem = [] if scalars is None else [pl.BlockSpec(memory_space=pltpu.SMEM)]
    held = [pltpu.with_memory_space_constraint(o, pltpu.VMEM) for o in operands]
    return pl.pallas_call(
        kernel,
        in_specs=smem + [vmem] * len(operands),
        out_specs=[vmem] * len(outs),
        out_shape=[(jax.ShapeDtypeStruct if place else pltpu.VMEM)(shape, kind) for shape, kind, *place in outs],
        cost_estimate=pl.CostEstimate(flops=flops, bytes_accessed=moved, transcendentals=0),
        compiler_params=pltpu.CompilerParams(vmem_limit_bytes=LIMIT),
    )(*([] if scalars is None else [scalars]), *held)


def columns(tint, t, away):
    return pl.ds(pl.multiple_of(t * 2048 + tint[away] * 512, 512), 512)


def diagonal():
    return lax.broadcasted_iota(jnp.int32, (16, 128), 0) == lax.broadcasted_iota(jnp.int32, (16, 128), 1)


def slots_kernel(rows, out):
    wide = rows[...].astype(F32)
    squares = jnp.sum(wide * wide, axis=1, keepdims=True)
    along = jnp.sum(jnp.where(diagonal(), squares, 0.0), axis=0, keepdims=True)
    extra = jnp.concatenate([*three_parts(along), jnp.zeros((5, 128), F32)], axis=0).astype(BF16)
    for chip, colour in enumerate(COLOURS):
        for i in range(4):
            start = colour * 512 + i * 128
            out[chip, i * 16 : (i + 1) * 16, :] = rows[:, start : start + 128]
        out[chip, 64:, :] = extra


def slots_call(rows):
    return call(slots_kernel, None, [rows], [((64, 72, 128), BF16, True)])[0]


def inverse_of(came, group):
    squares = sum(came[t * 16 + group, 64:, :].astype(F32) for t in range(4))
    along = jnp.sum(squares, axis=0, keepdims=True)
    squares = jnp.sum(jnp.where(diagonal(), along, 0.0), axis=1, keepdims=True)
    return lax.rsqrt(squares / 8192 + NORM_EPS)


def norm_kernel(came, gain, own):
    for group in range(16):
        span = slice(group * 16, (group + 1) * 16)
        inverse = inverse_of(came, group)
        for t in range(4):
            for i in range(4):
                unit = came[t * 16 + group, i * 16 : (i + 1) * 16, :].astype(F32) * inverse
                lanes = slice(i * 128, (i + 1) * 128)
                own[t, span, lanes] = (unit * gain[t : t + 1, lanes]).astype(BF16)


def norm_call(came, gain):
    return call(norm_kernel, None, [came, gain], [((4, 256, 512), BF16)], moved=2 << 20)[0]


def near_columns(t, away):
    return away * 4 + t


def early_kernel(tint, head, head_2, block, total, near, sems):
    copies = []
    for away in range(4):
        for t in range(4):
            at = near_columns(t, away)
            copies.append(pltpu.make_async_copy(head_2.at[:, columns(tint, t, away)], near.at[at], sems.at[at]))
            copies[-1].start()
    for t in range(4):
        part = lax.dot_general(head[:, columns(tint, t, 0)], block[t], NT, preferred_element_type=F32)
        total[:512, :] = part if t == 0 else total[:512, :] + part
    for t in range(4):
        copies[t].wait()
        part = lax.dot_general(near[near_columns(t, 0)], block[t], NT, preferred_element_type=F32)
        total[512:, :] = part if t == 0 else total[512:, :] + part
    for copy in copies[4:]:
        copy.wait()


def early_call(tint, head, head_2, block):
    vmem, anywhere = pl.BlockSpec(memory_space=pltpu.VMEM), pl.BlockSpec(memory_space=pl.ANY)
    return pl.pallas_call(
        early_kernel,
        in_specs=[pl.BlockSpec(memory_space=pltpu.SMEM), vmem, anywhere, vmem],
        out_specs=[vmem] * 2,
        out_shape=[pltpu.VMEM((1024, 256), F32), pltpu.VMEM((16, 512, 512), BF16)],
        scratch_shapes=[pltpu.SemaphoreType.DMA((16,))],
        cost_estimate=pl.CostEstimate(flops=2 * 1024 * 256 * 2048, bytes_accessed=9 << 20, transcendentals=0),
        compiler_params=pltpu.CompilerParams(vmem_limit_bytes=LIMIT),
    )(
        tint,
        pltpu.with_memory_space_constraint(head, pltpu.VMEM),
        pltpu.with_memory_space_constraint(head_2, pltpu.HBM),
        pltpu.with_memory_space_constraint(block, pltpu.VMEM),
    )


def last_kernel(tint, head, near, block_1, block_2, block_3, early, logits, lse, total):
    def step(t, first):
        for i in range(2):
            part = None
            for away, block in ((1, block_1), (2, block_2), (3, block_3)):
                side = near[near_columns(t, away)] if i else head[:, columns(tint, t, away)]
                term = lax.dot_general(side, block[t], NT, preferred_element_type=F32)
                part = term if part is None else part + term
            span = slice(i * 512, (i + 1) * 512)
            total[span, :] = part if first else total[span, :] + part

    step(0, True)

    @pl.loop(1, 4)
    def _(t):
        step(t, False)

    values = early[...] + total[...]
    logits[...] = values
    top = jnp.max(values, axis=0, keepdims=True)
    sums = top + jnp.log(jnp.sum(jnp.exp(values - top), axis=0, keepdims=True))
    sums = jnp.concatenate([sums[:, :128], sums[:, 128:]], axis=0)
    lse[...] = jnp.broadcast_to(sums[None], (64, 2, 128))


def last_call(tint, heads, blocks, early):
    outs = [((1024, 256), F32, jax.ShapeDtypeStruct), ((64, 2, 128), F32, jax.ShapeDtypeStruct), ((1024, 256), F32)]
    return call(last_kernel, tint, [*heads, *blocks, early], outs, 6 * 1024 * 256 * 2048, 17 << 20)[:2]


def product(tint, dlogits, heads, away, out):
    @pl.loop(0, 4)
    def _(t):
        value = jnp.dot(dlogits[:, :512], heads[0][:, columns(tint, t, away)], preferred_element_type=F32)
        value += jnp.dot(dlogits[:, 512:], heads[1][near_columns(t, away)], preferred_element_type=F32)
        out[t] = value.astype(out.dtype)


def turn_kernel(tint, logits, head, head_2, parts, labels, weights, turned, dlogits, inner, out, held, sem):
    copy = pltpu.make_async_copy(logits, held, sem)
    copy.start()
    lse = parts[...]
    top = jnp.max(lse, axis=0)
    log_total = top + jnp.log(jnp.sum(jnp.exp(lse - top[None]), axis=0))
    log_total = jnp.concatenate([log_total[:1], log_total[1:]], axis=1)
    copy.wait()
    for i in range(2):
        span = slice(i * 512, (i + 1) * 512)
        probs = jnp.exp(held[span, :] - log_total)
        ids = tint[5 + i] * 512 + lax.broadcasted_iota(jnp.int32, (512, 256), 0)
        hot = jnp.where(ids == labels[...], 1.0, 0.0)
        values = (weights[...] * (probs - hot)).astype(BF16)
        turned[span, :] = values
        dlogits[:, span] = values.T
        part = jnp.sum(values.astype(F32) * held[span, :], axis=0, keepdims=True)
        inner[...] = part if i == 0 else inner[...] + part
    product(tint, dlogits, (head, head_2), 1, out)


def turn_call(tint, logits, heads, parts, labels, weights):
    vmem = pl.BlockSpec(memory_space=pltpu.VMEM)
    return pl.pallas_call(
        turn_kernel,
        in_specs=[pl.BlockSpec(memory_space=pltpu.SMEM), pl.BlockSpec(memory_space=pl.ANY)] + [vmem] * 5,
        out_specs=[vmem] * 4,
        out_shape=[
            pltpu.VMEM((1024, 256), BF16),
            pltpu.VMEM((256, 1024), BF16),
            jax.ShapeDtypeStruct((1, 256), F32),
            pltpu.VMEM((4, 256, 512), BF16),
        ],
        scratch_shapes=[pltpu.VMEM((1024, 256), F32), pltpu.SemaphoreType.DMA],
        cost_estimate=pl.CostEstimate(flops=2 * 1024 * 256 * 2048, bytes_accessed=5 << 20, transcendentals=0),
        compiler_params=pltpu.CompilerParams(vmem_limit_bytes=LIMIT),
    )(tint, logits, *[pltpu.with_memory_space_constraint(h, pltpu.VMEM) for h in heads], parts, labels, weights)


def back_kernel(away, tint, dlogits, head, head_2, out):
    product(tint, dlogits, (head, head_2), away, out)


def back_call(tint, dlogits, heads, away, kind=BF16):
    kernel = functools.partial(back_kernel, away)
    return call(kernel, tint, [dlogits, *heads], [((4, 256, 512), kind)], 2 * 1024 * 256 * 2048, 4 << 20)[0]


def head_kernel(tint, turned, turned_2, *refs):
    out = refs[-1]
    for away in range(4):
        own, other = refs[away], refs[4 + away]
        value = jnp.dot(turned[...], own[0], preferred_element_type=F32)
        value += jnp.dot(turned_2[...], other[0], preferred_element_type=F32)
        out[:, pl.ds(pl.multiple_of(tint[away] * 512, 512), 512)] = value.astype(BF16)


def head_call(tint, turned, turned_2, own, other):
    block = pl.BlockSpec((1, 256, 512), lambda t, tint: (t, 0, 0))
    return pl.pallas_call(
        head_kernel,
        grid_spec=pltpu.PrefetchScalarGridSpec(
            num_scalar_prefetch=1,
            grid=(4,),
            in_specs=[pl.BlockSpec((512, 256), lambda t, tint: (0, 0))] * 2 + [block] * 8,
            out_specs=pl.BlockSpec((512, 2048), lambda t, tint: (0, t)),
        ),
        out_shape=jax.ShapeDtypeStruct((512, 8192), BF16),
        cost_estimate=pl.CostEstimate(flops=2 * 512 * 512 * 8192, bytes_accessed=17 << 20, transcendentals=0),
        compiler_params=pltpu.CompilerParams(vmem_limit_bytes=LIMIT),
    )(tint, turned, turned_2, *own, *other)


def three_parts(value):
    high = value.astype(BF16).astype(F32)
    middle = (value - high).astype(BF16).astype(F32)
    return high, middle, value - high - middle


def join_kernel(came, ours, one, two, three, inner, out, inverse_rms, slots, sems):
    for group in range(16):
        inverse_rms[group * 16 : (group + 1) * 16, :] = jnp.broadcast_to(inverse_of(came, group), (16, 128))
    products = [part[i : i + 1] for part in three_parts(inner[...]) for i in range(2)]
    copies = []
    for t in range(4):
        gain = jnp.zeros((1, 512), F32)
        for group in range(16):
            span = slice(group * 16, (group + 1) * 16)
            total = ours[t, span] + one[t, span].astype(F32) + two[t, span].astype(F32) + three[t, span].astype(F32)
            slots[t * 16 + group, :, :512] = total.astype(BF16)
            pieces = [came[t * 16 + group, i * 16 : (i + 1) * 16, :] for i in range(4)]
            unit = jnp.concatenate(pieces, axis=1).astype(F32) * inverse_rms[span, :1]
            gain += jnp.sum(total * unit, axis=0, keepdims=True)
        parts = [part[:, i * 128 : (i + 1) * 128] for part in three_parts(gain)[:2] for i in range(4)]
        extra = jnp.concatenate(parts + products + [jnp.zeros((2, 128), F32)], axis=0).astype(BF16)
        for group in range(16):
            slots[t * 16 + group, :, 512:] = extra
        span = pl.ds(t * 16, 16)
        copies.append(pltpu.make_async_copy(slots.at[span], out.at[span], sems.at[t]))
        copies[-1].start()
    for copy in copies:
        copy.wait()


def join_call(*operands):
    vmem = pl.BlockSpec(memory_space=pltpu.VMEM)
    return pl.pallas_call(
        join_kernel,
        in_specs=[vmem] * len(operands),
        out_specs=[pl.BlockSpec(memory_space=pl.ANY), vmem],
        out_shape=[pltpu.HBM((64, 16, 640), BF16), pltpu.VMEM((256, 128), F32)],
        scratch_shapes=[pltpu.VMEM((64, 16, 640), BF16), pltpu.SemaphoreType.DMA((4,))],
        cost_estimate=pl.CostEstimate(flops=0, bytes_accessed=6 << 20, transcendentals=0),
        compiler_params=pltpu.CompilerParams(vmem_limit_bytes=LIMIT),
    )(*[pltpu.with_memory_space_constraint(o, pltpu.VMEM) for o in operands])


def tail_kernel(info, terms, rows, inverse_rms, gain, placed, gain_grad):
    sums = [None] * 4
    for chip, colour in enumerate(COLOURS):
        term = terms[chip].astype(F32)
        sums[colour] = term if sums[colour] is None else sums[colour] + term
    products = sum(s[8:14, 512:] for s in sums)
    lane = lax.broadcasted_iota(jnp.int32, (16, 128), 1)
    row = info[2] * 16 + lax.broadcasted_iota(jnp.int32, (16, 128), 0)
    here = [jnp.where(lane + 128 * (i % 2) == row, products[i : i + 1], 0.0) for i in range(6)]
    inner = jnp.sum(sum(here), axis=1, keepdims=True) / 8192
    inverse = inverse_rms[:, :1]
    for colour, total in enumerate(sums):
        span = slice(colour * 512, (colour + 1) * 512)
        gain_grad[colour * 4 : (colour + 1) * 4, :] = total[:4, 512:] + total[4:8, 512:]
        unit = rows[:, span].astype(F32) * inverse
        exit_grad = inverse * (total[:, :512] * gain[:, span] - unit * inner)
        for section in range(16):
            value = jnp.where(info[0] == section, exit_grad[:8], jnp.where(info[1] == section, exit_grad[8:], 0.0))
            placed[section, :, span] = value.astype(BF16)


def tail_call(info, *operands):
    outs = [((16, 8, 2048), BF16, True), ((16, 128), F32)]
    return call(tail_kernel, info, operands, outs, moved=2 << 20)


def hold_kernel(source, out):
    out[...] = source[...]


def add_kernel(exits, from_next, out):
    out[...] = (exits[...].astype(F32) + from_next[...].astype(F32)).astype(BF16)


def local(hidden, section_cotangent, norm_gain, head, labels, loss_mask, exit_on):
    core, x, y, zl, zh = (lax.axis_index(a) for a in ("c", "x", "y", "zl", "zh"))
    device = lax.axis_index(AXES).astype(jnp.int32)
    colour = (x + 2 * y + 3 * (2 * zh + zl)) % 4
    aways = (colour + jnp.arange(4, dtype=jnp.int32)) % 4
    tint = jnp.concatenate([aways, core.reshape(1), device.reshape(1), (device + 8 - 16 * core).reshape(1)]).astype(jnp.int32)

    heads = [head, other_core(head)]
    came = lax.all_to_all(hidden.reshape(16, 8, 2048), PIPE, 0, 0, tiled=True)
    section_ids = jnp.arange(16, dtype=jnp.int32)
    first = jnp.min(jnp.where(exit_on == 1, section_ids, 16))
    second = jnp.max(jnp.where(exit_on == 1, section_ids, -1))
    chosen = jnp.stack([first, second])
    scores = (chosen + 1).astype(F32)
    weights = scores / jnp.sum(scores)

    rows = jnp.concatenate([lax.dynamic_index_in_dim(came, s, 0, False) for s in (first, second)])
    norm_gain, rows = lax.optimization_barrier((norm_gain, rows))
    turns = [norm_gain] + [move(norm_gain, lambda y, z, c, x, k=k: (y, z, c, x + k)) for k in (1, 2, 3)]
    ring = jnp.stack(turns[::-1] * 2)
    gain = lax.dynamic_slice(ring, ((3 - x) % 4, colour * 512), (4, 512))
    token_info, rows = lax.optimization_barrier((jnp.stack([labels, loss_mask]), rows))
    other_info = move(token_info, lambda y, z, c, x: (y, z + 2, c, x))
    both = jnp.where(zh == 0, jnp.stack([token_info, other_info]), jnp.stack([other_info, token_info]))
    by_row = jnp.broadcast_to(
        both.reshape(2, 2, 4, 2, 2, 8).transpose(4, 1, 2, 3, 0, 5)[:, :, :, :, :, None], (2, 2, 4, 2, 2, 2, 8)
    )
    by_row = jnp.where(core == 0, by_row[0], by_row[1])
    row_labels = by_row[0].reshape(1, 256)
    row_weights = (weights[:, None] * by_row[1].astype(F32)).reshape(1, 256)

    quarter = lax.all_to_all(slots_call(rows), CHIPS, 0, 0, tiled=True)
    quarter, row_labels, row_weights, gain = lax.optimization_barrier((quarter, row_labels, row_weights, gain))
    own = norm_call(quarter, gain)

    blocks = [own, to_colour(own, 3), to_colour(own, 2), to_colour(own, 1)]
    early, near = early_call(tint, *heads, own)
    heads = [head, near]
    *blocks[1:], early = lax.optimization_barrier((*blocks[1:], early))
    logits, lse = last_call(tint, heads, blocks[1:], early)
    parts = lax.all_to_all(lse, CHIPS, 0, 0, tiled=True)
    turned, dlogits, inner, product_1 = turn_call(tint, logits, heads, parts, row_labels, row_weights)

    sums = [product_1] + [back_call(tint, dlogits, heads, away) for away in (2, 3)]
    arrived = [to_colour(s, away) for s, away in zip(sums, (1, 2, 3))]
    late, _ = lax.optimization_barrier((dlogits, sums[2]))
    ours = back_call(tint, late, heads, 0, F32)
    ours, turned, *blocks = lax.optimization_barrier((ours, turned, *blocks))
    turned_2 = other_core(turned[512:])
    mates = [other_core(b) for b in blocks]
    inner = inner.reshape(2, 128)
    slots, inverse_rms = join_call(quarter, ours, *arrived, inner)
    terms = lax.all_to_all(slots, CHIPS, 0, 0, tiled=True)
    head_grad = head_call(tint, turned[:512], turned_2, blocks, mates)
    place = (y * 2 + zl) * 2 + zh
    inverse_here = lax.dynamic_slice_in_dim(inverse_rms, place * 16, 16, 0)
    terms, head_grad, inverse_here = lax.optimization_barrier((terms, head_grad, inverse_here))
    info = jnp.concatenate([chosen, place.reshape(1)]).astype(jnp.int32)
    placed, gain_grad = tail_call(info, terms, rows, inverse_here, norm_gain.reshape(1, 2048))
    came = lax.all_to_all(placed, PIPE, 0, 0, tiled=True)
    gain_grad = (gain_grad + other_core(gain_grad)).reshape(2048)
    from_next = move(section_cotangent, back_one)
    from_next = call(hold_kernel, None, [from_next[0]], [((128, 2048), BF16)])[0]
    residual_grad = call(add_kernel, None, [came.reshape(128, 2048), from_next], [((128, 2048), BF16, True)])[0][None]
    return head_grad, residual_grad, gain_grad


def solution(mesh):
    fine = Mesh(mesh.devices.reshape(SIZES), AXES)
    in_specs = (
        P(PIPE, "zh", "x"),
        P(PIPE, "zh", "x"),
        P("x"),
        P(AXES, None),
        P("zh"),
        P("zh"),
        P(),
    )
    out_specs = (P(AXES, None), P(PIPE, "zh", "x"), P("x"))
    return jax.shard_map(local, mesh=fine, in_specs=in_specs, out_specs=out_specs, check_vma=False)
```

```python
import functools

import jax
import jax.numpy as jnp
import numpy as np
from jax import lax
from jax.experimental import pallas as pl
from jax.experimental.pallas import tpu as pltpu
from jax.sharding import Mesh, PartitionSpec as P

NORM_EPS = 1e-05
AXES = ("y", "zl", "c", "x", "zh")
SIZES = (4, 2, 2, 4, 2)
CHIPS = ("x", "y", "zl", "zh")
PIPE = ("y", "zl", "c")
F32, BF16 = jnp.float32, jnp.bfloat16
NT = (((1,), (1,)), ((), ()))
LIMIT = 16 << 20
COLOURS = [(x + 2 * y + 3 * (2 * zh + zl)) % 4 for x in range(4) for y in range(4) for zl in range(2) for zh in range(2)]


def route(step):
    pairs = []
    for source in range(128):
        y, zl, c, x, zh = (int(i) for i in np.unravel_index(source, SIZES))
        there = step(y, 2 * zh + zl, c, x)
        if there is not None:
            y, z, c, x = there[0] % 4, there[1] % 4, there[2] % 2, there[3] % 4
            pairs.append((source, int(np.ravel_multi_index((y, z % 2, c, x, z // 2), SIZES))))
    return pairs


def move(block, step):
    return lax.ppermute(block, AXES, route(step))


def other_core(block):
    return move(block, lambda y, z, c, x: (y, z, 1 - c, x))


def to_colour(block, away):
    if away == 1:
        return move(block, lambda y, z, c, x: (y, z - 1, c, x) if c else (y, z, c, x + 1))
    if away == 3:
        return move(block, lambda y, z, c, x: (y, z + 1, c, x) if c else (y, z, c, x - 1))
    return move(block, lambda y, z, c, x: (y - 1 if c else y + 1, z, c, x))


def back_one(y, z, c, x):
    section = (y * 2 + z % 2) * 2 + c - 1
    return None if section < 0 else (section // 4, z // 2 * 2 + section // 2 % 2, section % 2, x)


def call(kernel, scalars, operands, outs, flops=0, moved=1 << 20):
    vmem = pl.BlockSpec(memory_space=pltpu.VMEM)
    smem = [] if scalars is None else [pl.BlockSpec(memory_space=pltpu.SMEM)]
    held = [pltpu.with_memory_space_constraint(o, pltpu.VMEM) for o in operands]
    return pl.pallas_call(
        kernel,
        in_specs=smem + [vmem] * len(operands),
        out_specs=[vmem] * len(outs),
        out_shape=[(jax.ShapeDtypeStruct if place else pltpu.VMEM)(shape, kind) for shape, kind, *place in outs],
        cost_estimate=pl.CostEstimate(flops=flops, bytes_accessed=moved, transcendentals=0),
        compiler_params=pltpu.CompilerParams(vmem_limit_bytes=LIMIT),
    )(*([] if scalars is None else [scalars]), *held)


def columns(tint, t, away):
    return pl.ds(pl.multiple_of(t * 2048 + tint[away] * 512, 512), 512)


def diagonal():
    return lax.broadcasted_iota(jnp.int32, (16, 128), 0) == lax.broadcasted_iota(jnp.int32, (16, 128), 1)


def slots_kernel(rows, out):
    wide = rows[...].astype(F32)
    squares = jnp.sum(wide * wide, axis=1, keepdims=True)
    along = jnp.sum(jnp.where(diagonal(), squares, 0.0), axis=0, keepdims=True)
    extra = jnp.concatenate([*three_parts(along), jnp.zeros((5, 128), F32)], axis=0).astype(BF16)
    for chip, colour in enumerate(COLOURS):
        for i in range(4):
            start = colour * 512 + i * 128
            out[chip, i * 16 : (i + 1) * 16, :] = rows[:, start : start + 128]
        out[chip, 64:, :] = extra


def slots_call(rows):
    return call(slots_kernel, None, [rows], [((64, 72, 128), BF16, True)])[0]


def inverse_of(came, group):
    squares = sum(came[t * 16 + group, 64:, :].astype(F32) for t in range(4))
    along = jnp.sum(squares, axis=0, keepdims=True)
    squares = jnp.sum(jnp.where(diagonal(), along, 0.0), axis=1, keepdims=True)
    return lax.rsqrt(squares / 8192 + NORM_EPS)


def norm_kernel(came, gain, own):
    for group in range(16):
        span = slice(group * 16, (group + 1) * 16)
        inverse = inverse_of(came, group)
        for t in range(4):
            for i in range(4):
                unit = came[t * 16 + group, i * 16 : (i + 1) * 16, :].astype(F32) * inverse
                lanes = slice(i * 128, (i + 1) * 128)
                own[t, span, lanes] = (unit * gain[t : t + 1, lanes]).astype(BF16)


def norm_call(came, gain):
    return call(norm_kernel, None, [came, gain], [((4, 256, 512), BF16)], moved=2 << 20)[0]


def near_columns(t, away):
    return away * 4 + t


def early_kernel(tint, head, head_2, block, total, near, sems):
    copies = {}
    for away in range(4):
        for t in range(4):
            at = near_columns(t, away)
            for i, source in enumerate((head, head_2)):
                out = near.at[at, pl.ds(i * 512, 512)]
                copy = pltpu.make_async_copy(source.at[:, columns(tint, t, away)], out, sems.at[i * 16 + at])
                copy.start()
                copies[i, at] = copy
    for t in range(4):
        at = near_columns(t, 0)
        copies[0, at].wait()
        copies[1, at].wait()
        part = lax.dot_general(near[at], block[t], NT, preferred_element_type=F32)
        total[...] = part if t == 0 else total[...] + part
    for away in range(1, 4):
        for t in range(4):
            for i in range(2):
                copies[i, near_columns(t, away)].wait()


def early_call(tint, head, head_2, block):
    vmem, anywhere = pl.BlockSpec(memory_space=pltpu.VMEM), pl.BlockSpec(memory_space=pl.ANY)
    return pl.pallas_call(
        early_kernel,
        in_specs=[pl.BlockSpec(memory_space=pltpu.SMEM), anywhere, anywhere, vmem],
        out_specs=[vmem] * 2,
        out_shape=[pltpu.VMEM((1024, 256), F32), pltpu.VMEM((16, 1024, 512), BF16)],
        scratch_shapes=[pltpu.SemaphoreType.DMA((32,))],
        cost_estimate=pl.CostEstimate(flops=2 * 1024 * 256 * 2048, bytes_accessed=17 << 20, transcendentals=0),
        compiler_params=pltpu.CompilerParams(vmem_limit_bytes=LIMIT),
    )(
        tint,
        pltpu.with_memory_space_constraint(head, pltpu.HBM),
        pltpu.with_memory_space_constraint(head_2, pltpu.HBM),
        pltpu.with_memory_space_constraint(block, pltpu.VMEM),
    )


def last_kernel(tint, near, block_1, block_2, block_3, early, logits, lse, total):
    def part(t):
        return sum(
            lax.dot_general(near[near_columns(t, away)], block[t], NT, preferred_element_type=F32)
            for away, block in ((1, block_1), (2, block_2), (3, block_3))
        )

    total[...] = part(0)

    @pl.loop(1, 4)
    def _(t):
        total[...] += part(t)

    values = early[...] + total[...]
    logits[...] = values
    top = jnp.max(values, axis=0, keepdims=True)
    sums = top + jnp.log(jnp.sum(jnp.exp(values - top), axis=0, keepdims=True))
    sums = jnp.concatenate([sums[:, :128], sums[:, 128:]], axis=0)
    lse[...] = jnp.broadcast_to(sums[None], (64, 2, 128))


def last_call(tint, near, blocks, early):
    outs = [((1024, 256), F32, jax.ShapeDtypeStruct), ((64, 2, 128), F32, jax.ShapeDtypeStruct), ((1024, 256), F32)]
    return call(last_kernel, tint, [near, *blocks, early], outs, 6 * 1024 * 256 * 2048, 17 << 20)[:2]


def product(dlogits, near, away, out):
    @pl.loop(0, 4)
    def _(t):
        out[t] = jnp.dot(dlogits[...], near[near_columns(t, away)], preferred_element_type=F32).astype(out.dtype)


def turn_kernel(tint, logits, near, parts, labels, weights, turned, turned_2, dlogits, inner, out, held, sem):
    copy = pltpu.make_async_copy(logits, held, sem)
    copy.start()
    lse = parts[...]
    top = jnp.max(lse, axis=0)
    log_total = top + jnp.log(jnp.sum(jnp.exp(lse - top[None]), axis=0))
    log_total = jnp.concatenate([log_total[:1], log_total[1:]], axis=1)
    copy.wait()
    for i in range(2):
        span = slice(i * 512, (i + 1) * 512)
        probs = jnp.exp(held[span, :] - log_total)
        ids = tint[5 + i] * 512 + lax.broadcasted_iota(jnp.int32, (512, 256), 0)
        hot = jnp.where(ids == labels[...], 1.0, 0.0)
        values = (weights[...] * (probs - hot)).astype(BF16)
        (turned, turned_2)[i][...] = values
        dlogits[:, span] = values.T
        part = jnp.sum(values.astype(F32) * held[span, :], axis=0, keepdims=True)
        inner[...] = part if i == 0 else inner[...] + part
    product(dlogits, near, 1, out)


def turn_call(tint, logits, near, parts, labels, weights):
    vmem = pl.BlockSpec(memory_space=pltpu.VMEM)
    return pl.pallas_call(
        turn_kernel,
        in_specs=[pl.BlockSpec(memory_space=pltpu.SMEM), pl.BlockSpec(memory_space=pl.ANY)] + [vmem] * 4,
        out_specs=[vmem] * 5,
        out_shape=[
            pltpu.VMEM((512, 256), BF16),
            pltpu.VMEM((512, 256), BF16),
            pltpu.VMEM((256, 1024), BF16),
            jax.ShapeDtypeStruct((1, 256), F32),
            pltpu.VMEM((4, 256, 512), BF16),
        ],
        scratch_shapes=[pltpu.VMEM((1024, 256), F32), pltpu.SemaphoreType.DMA],
        cost_estimate=pl.CostEstimate(flops=2 * 1024 * 256 * 2048, bytes_accessed=5 << 20, transcendentals=0),
        compiler_params=pltpu.CompilerParams(vmem_limit_bytes=LIMIT),
    )(tint, logits, pltpu.with_memory_space_constraint(near, pltpu.VMEM), parts, labels, weights)


def back_kernel(away, dlogits, near, out):
    product(dlogits, near, away, out)


def back_call(dlogits, near, away, kind=BF16):
    kernel = functools.partial(back_kernel, away)
    return call(kernel, None, [dlogits, near], [((4, 256, 512), kind)], 2 * 1024 * 256 * 2048, 4 << 20)[0]


def head_kernel(tint, turned, turned_2, *refs):
    out = refs[-1]
    for away in range(4):
        own, other = refs[away], refs[4 + away]
        value = jnp.dot(turned[...], own[0], preferred_element_type=F32)
        value += jnp.dot(turned_2[...], other[0], preferred_element_type=F32)
        out[:, pl.ds(pl.multiple_of(tint[away] * 512, 512), 512)] = value.astype(BF16)


def head_call(tint, turned, turned_2, own, other):
    block = pl.BlockSpec((1, 256, 512), lambda t, tint: (t, 0, 0))
    return pl.pallas_call(
        head_kernel,
        grid_spec=pltpu.PrefetchScalarGridSpec(
            num_scalar_prefetch=1,
            grid=(4,),
            in_specs=[pl.BlockSpec((512, 256), lambda t, tint: (0, 0))] * 2 + [block] * 8,
            out_specs=pl.BlockSpec((512, 2048), lambda t, tint: (0, t)),
        ),
        out_shape=jax.ShapeDtypeStruct((512, 8192), BF16),
        cost_estimate=pl.CostEstimate(flops=2 * 512 * 512 * 8192, bytes_accessed=17 << 20, transcendentals=0),
        compiler_params=pltpu.CompilerParams(vmem_limit_bytes=LIMIT),
    )(tint, turned, turned_2, *own, *other)


def three_parts(value):
    high = value.astype(BF16).astype(F32)
    middle = (value - high).astype(BF16).astype(F32)
    return high, middle, value - high - middle


def join_kernel(came, ours, one, two, three, inner, out, inverse_rms, slots, sems):
    for group in range(16):
        inverse_rms[group * 16 : (group + 1) * 16, :] = jnp.broadcast_to(inverse_of(came, group), (16, 128))
    products = [part[i : i + 1] for part in three_parts(inner[...]) for i in range(2)]
    copies = []
    for t in range(4):
        gain = jnp.zeros((1, 512), F32)
        for group in range(16):
            span = slice(group * 16, (group + 1) * 16)
            total = ours[t, span] + one[t, span].astype(F32) + two[t, span].astype(F32) + three[t, span].astype(F32)
            for i in range(4):
                slots[t * 16 + group, i * 16 : (i + 1) * 16, :] = total[:, i * 128 : (i + 1) * 128].astype(BF16)
            pieces = [came[t * 16 + group, i * 16 : (i + 1) * 16, :] for i in range(4)]
            unit = jnp.concatenate(pieces, axis=1).astype(F32) * inverse_rms[span, :1]
            gain += jnp.sum(total * unit, axis=0, keepdims=True)
        high, middle, _ = three_parts(gain)
        for share in range(8):
            part = jnp.concatenate([p[:, share * 64 : (share + 1) * 64] for p in (high, middle)], axis=1)
            extra = jnp.concatenate([part] + products + [jnp.zeros((1, 128), F32)], axis=0).astype(BF16)
            slots[t * 16 + share * 2, 64:, :] = extra
            slots[t * 16 + share * 2 + 1, 64:, :] = extra
        span = pl.ds(t * 16, 16)
        copies.append(pltpu.make_async_copy(slots.at[span], out.at[span], sems.at[t]))
        copies[-1].start()
    for copy in copies:
        copy.wait()


def join_call(*operands):
    vmem = pl.BlockSpec(memory_space=pltpu.VMEM)
    return pl.pallas_call(
        join_kernel,
        in_specs=[vmem] * len(operands),
        out_specs=[pl.BlockSpec(memory_space=pl.ANY), vmem],
        out_shape=[pltpu.HBM((64, 72, 128), BF16), pltpu.VMEM((256, 128), F32)],
        scratch_shapes=[pltpu.VMEM((64, 72, 128), BF16), pltpu.SemaphoreType.DMA((4,))],
        cost_estimate=pl.CostEstimate(flops=0, bytes_accessed=6 << 20, transcendentals=0),
        compiler_params=pltpu.CompilerParams(vmem_limit_bytes=LIMIT),
    )(*[pltpu.with_memory_space_constraint(o, pltpu.VMEM) for o in operands])


def tail_kernel(info, terms, rows, inverse_rms, gain, placed):
    sums, extra = [[None] * 4 for _ in range(4)], [None] * 4
    for chip, colour in enumerate(COLOURS):
        for i in range(4):
            term = terms[chip, i * 16 : (i + 1) * 16, :].astype(F32)
            sums[colour][i] = term if sums[colour][i] is None else sums[colour][i] + term
        term = terms[chip, 64:, :].astype(F32)
        extra[colour] = term if extra[colour] is None else extra[colour] + term
    products = sum(extra)[1:7]
    lane = lax.broadcasted_iota(jnp.int32, (16, 128), 1)
    row = info[2] * 16 + lax.broadcasted_iota(jnp.int32, (16, 128), 0)
    here = [jnp.where(lane + 128 * (i % 2) == row, products[i : i + 1], 0.0) for i in range(6)]
    inner = jnp.sum(sum(here), axis=1, keepdims=True) / 8192
    inverse = inverse_rms[:, :1]
    share = jnp.concatenate([e[:1, :64] + e[:1, 64:] for e in extra], axis=1)
    parts = [part[:, i * 128 : (i + 1) * 128] for part in three_parts(share)[:2] for i in range(2)]
    beside = jnp.concatenate(parts + [jnp.zeros((4, 128), F32)], axis=0).astype(BF16)
    for section in range(16):
        placed[section, :, 2048:] = beside
    for colour in range(4):
        span = slice(colour * 512, (colour + 1) * 512)
        unit = rows[:, span].astype(F32) * inverse
        total = jnp.concatenate(sums[colour], axis=1)
        exit_grad = inverse * (total * gain[:, span] - unit * inner)
        for section in range(16):
            value = jnp.where(info[0] == section, exit_grad[:8], jnp.where(info[1] == section, exit_grad[8:], 0.0))
            placed[section, :, span] = value.astype(BF16)


def tail_call(info, *operands):
    outs = [((16, 8, 2176), BF16, True)]
    return call(tail_kernel, info, operands, outs, moved=2 << 20)[0]


def hold_kernel(source, out):
    out[...] = source[...]


def add_kernel(exits, from_next, out):
    out[...] = (exits[:, :, :2048].astype(F32) + from_next[...].astype(F32)).astype(BF16)


def local(hidden, section_cotangent, norm_gain, head, labels, loss_mask, exit_on):
    core, x, y, zl, zh = (lax.axis_index(a) for a in ("c", "x", "y", "zl", "zh"))
    device = lax.axis_index(AXES).astype(jnp.int32)
    colour = (x + 2 * y + 3 * (2 * zh + zl)) % 4
    aways = (colour + jnp.arange(4, dtype=jnp.int32)) % 4
    tint = jnp.concatenate([aways, core.reshape(1), device.reshape(1), (device + 8 - 16 * core).reshape(1)]).astype(jnp.int32)

    head_2 = other_core(head)
    came = lax.all_to_all(hidden.reshape(16, 8, 2048), PIPE, 0, 0, tiled=True)
    section_ids = jnp.arange(16, dtype=jnp.int32)
    first = jnp.min(jnp.where(exit_on == 1, section_ids, 16))
    second = jnp.max(jnp.where(exit_on == 1, section_ids, -1))
    chosen = jnp.stack([first, second])
    scores = (chosen + 1).astype(F32)
    weights = scores / jnp.sum(scores)

    rows = jnp.concatenate([lax.dynamic_index_in_dim(came, s, 0, False) for s in (first, second)])
    norm_gain, rows = lax.optimization_barrier((norm_gain, rows))
    turns = [norm_gain] + [move(norm_gain, lambda y, z, c, x, k=k: (y, z, c, x + k)) for k in (1, 2, 3)]
    ring = jnp.stack(turns[::-1] * 2)
    gain = lax.dynamic_slice(ring, ((3 - x) % 4, colour * 512), (4, 512))
    token_info, rows = lax.optimization_barrier((jnp.stack([labels, loss_mask]), rows))
    other_info = move(token_info, lambda y, z, c, x: (y, z + 2, c, x))
    both = jnp.where(zh == 0, jnp.stack([token_info, other_info]), jnp.stack([other_info, token_info]))
    by_row = jnp.broadcast_to(
        both.reshape(2, 2, 4, 2, 2, 8).transpose(4, 1, 2, 3, 0, 5)[:, :, :, :, :, None], (2, 2, 4, 2, 2, 2, 8)
    )
    by_row = jnp.where(core == 0, by_row[0], by_row[1])
    row_labels = by_row[0].reshape(1, 256)
    row_weights = (weights[:, None] * by_row[1].astype(F32)).reshape(1, 256)

    quarter = lax.all_to_all(slots_call(rows), CHIPS, 0, 0, tiled=True)
    quarter, row_labels, row_weights, gain = lax.optimization_barrier((quarter, row_labels, row_weights, gain))
    own = norm_call(quarter, gain)

    blocks = [own, to_colour(own, 3), to_colour(own, 2), to_colour(own, 1)]
    early, near = early_call(tint, head, head_2, own)
    *blocks[1:], early = lax.optimization_barrier((*blocks[1:], early))
    logits, lse = last_call(tint, near, blocks[1:], early)
    parts = lax.all_to_all(lse, CHIPS, 0, 0, tiled=True)
    turned, turned_2, dlogits, inner, product_1 = turn_call(tint, logits, near, parts, row_labels, row_weights)

    sums = [product_1] + [back_call(dlogits, near, away) for away in (2, 3)]
    arrived = [to_colour(s, away) for s, away in zip(sums, (1, 2, 3))]
    late, _ = lax.optimization_barrier((dlogits, sums[2]))
    ours = back_call(late, near, 0, F32)
    turned_2 = other_core(turned_2)
    ours, turned_2, *blocks = lax.optimization_barrier((ours, turned_2, *blocks))
    mates = [other_core(b) for b in blocks]
    inner = inner.reshape(2, 128)
    slots, inverse_rms = join_call(quarter, ours, *arrived, inner)
    terms = lax.all_to_all(slots, CHIPS, 0, 0, tiled=True)
    head_grad = head_call(tint, turned, turned_2, blocks, mates)
    place = (y * 2 + zl) * 2 + zh
    inverse_here = lax.dynamic_slice_in_dim(inverse_rms, place * 16, 16, 0)
    terms, head_grad, inverse_here = lax.optimization_barrier((terms, head_grad, inverse_here))
    info = jnp.concatenate([chosen, place.reshape(1)]).astype(jnp.int32)
    placed = tail_call(info, terms, rows, inverse_here, norm_gain.reshape(1, 2048))
    came = lax.all_to_all(placed, PIPE, 0, 0, tiled=True)
    from_next = move(section_cotangent, back_one)
    from_next = call(hold_kernel, None, [from_next.reshape(16, 8, 2048)], [((16, 8, 2048), BF16)])[0]
    residual_grad = call(add_kernel, None, [came, from_next], [((16, 8, 2048), BF16, True)])[0].reshape(1, 128, 2048)
    came, residual_grad = lax.optimization_barrier((came, residual_grad))
    shares = came[:, :4, 2048:].astype(F32).reshape(8, 2, 2, 4, 64)
    gain_grad = jnp.sum(shares, axis=(1, 2)).transpose(1, 0, 2).reshape(2048)
    return head_grad, residual_grad, gain_grad


def solution(mesh):
    fine = Mesh(mesh.devices.reshape(SIZES), AXES)
    in_specs = (
        P(PIPE, "zh", "x"),
        P(PIPE, "zh", "x"),
        P("x"),
        P(AXES, None),
        P("zh"),
        P("zh"),
        P(),
    )
    out_specs = (P(AXES, None), P(PIPE, "zh", "x"), P("x"))
    return jax.shard_map(local, mesh=fine, in_specs=in_specs, out_specs=out_specs, check_vma=False)
```

```python
import functools

import jax
import jax.numpy as jnp
import numpy as np
from jax import lax
from jax.experimental import pallas as pl
from jax.experimental.pallas import tpu as pltpu
from jax.sharding import Mesh, PartitionSpec as P

NORM_EPS = 1e-05
AXES = ("y", "zl", "c", "x", "zh")
SIZES = (4, 2, 2, 4, 2)
CHIPS = ("x", "y", "zl", "zh")
PIPE = ("y", "zl", "c")
F32, BF16 = jnp.float32, jnp.bfloat16
NT = (((1,), (1,)), ((), ()))
LIMIT = 16 << 20
COLOURS = [(x + 2 * y + 3 * (2 * zh + zl)) % 4 for x in range(4) for y in range(4) for zl in range(2) for zh in range(2)]


def route(step):
    pairs = []
    for source in range(128):
        y, zl, c, x, zh = (int(i) for i in np.unravel_index(source, SIZES))
        there = step(y, 2 * zh + zl, c, x)
        if there is not None:
            y, z, c, x = there[0] % 4, there[1] % 4, there[2] % 2, there[3] % 4
            pairs.append((source, int(np.ravel_multi_index((y, z % 2, c, x, z // 2), SIZES))))
    return pairs


def move(block, step):
    return lax.ppermute(block, AXES, route(step))


def other_core(block):
    return move(block, lambda y, z, c, x: (y, z, 1 - c, x))


def to_colour(block, away):
    if away == 1:
        return move(block, lambda y, z, c, x: (y, z - 1, c, x) if c else (y, z, c, x + 1))
    if away == 3:
        return move(block, lambda y, z, c, x: (y, z + 1, c, x) if c else (y, z, c, x - 1))
    return move(block, lambda y, z, c, x: (y - 1 if c else y + 1, z, c, x))


def back_one(y, z, c, x):
    section = (y * 2 + z % 2) * 2 + c - 1
    return None if section < 0 else (section // 4, z // 2 * 2 + section // 2 % 2, section % 2, x)


def call(kernel, scalars, operands, outs, flops=0, moved=1 << 20):
    vmem = pl.BlockSpec(memory_space=pltpu.VMEM)
    smem = [] if scalars is None else [pl.BlockSpec(memory_space=pltpu.SMEM)]
    held = [pltpu.with_memory_space_constraint(o, pltpu.VMEM) for o in operands]
    return pl.pallas_call(
        kernel,
        in_specs=smem + [vmem] * len(operands),
        out_specs=[vmem] * len(outs),
        out_shape=[(jax.ShapeDtypeStruct if place else pltpu.VMEM)(shape, kind) for shape, kind, *place in outs],
        cost_estimate=pl.CostEstimate(flops=flops, bytes_accessed=moved, transcendentals=0),
        compiler_params=pltpu.CompilerParams(vmem_limit_bytes=LIMIT),
    )(*([] if scalars is None else [scalars]), *held)


def columns(tint, t, away):
    return pl.ds(pl.multiple_of(t * 2048 + tint[away] * 512, 512), 512)


def diagonal():
    return lax.broadcasted_iota(jnp.int32, (16, 128), 0) == lax.broadcasted_iota(jnp.int32, (16, 128), 1)


def slots_kernel(rows, out):
    wide = rows[...].astype(F32)
    squares = jnp.sum(wide * wide, axis=1, keepdims=True)
    along = jnp.sum(jnp.where(diagonal(), squares, 0.0), axis=0, keepdims=True)
    extra = jnp.concatenate([*three_parts(along), jnp.zeros((5, 128), F32)], axis=0).astype(BF16)
    for chip, colour in enumerate(COLOURS):
        for i in range(4):
            start = colour * 512 + i * 128
            out[chip, i * 16 : (i + 1) * 16, :] = rows[:, start : start + 128]
        out[chip, 64:, :] = extra


def slots_call(rows):
    return call(slots_kernel, None, [rows], [((64, 72, 128), BF16, True)])[0]


def inverse_of(came, group):
    squares = sum(came[t * 16 + group, 64:, :].astype(F32) for t in range(4))
    along = jnp.sum(squares, axis=0, keepdims=True)
    squares = jnp.sum(jnp.where(diagonal(), along, 0.0), axis=1, keepdims=True)
    return lax.rsqrt(squares / 8192 + NORM_EPS)


def norm_kernel(came, gain, own):
    for group in range(16):
        span = slice(group * 16, (group + 1) * 16)
        inverse = inverse_of(came, group)
        for t in range(4):
            for i in range(4):
                unit = came[t * 16 + group, i * 16 : (i + 1) * 16, :].astype(F32) * inverse
                lanes = slice(i * 128, (i + 1) * 128)
                own[t, span, lanes] = (unit * gain[t : t + 1, lanes]).astype(BF16)


def norm_call(came, gain):
    return call(norm_kernel, None, [came, gain], [((4, 256, 512), BF16)], moved=2 << 20)[0]


def near_columns(t, away):
    return away * 4 + t


def early_kernel(tint, head, head_2, block, total, near, sems):
    copies = {}
    for away in range(4):
        for t in range(4):
            at = near_columns(t, away)
            for i, source in enumerate((head, head_2)):
                out = near.at[at, pl.ds(i * 512, 512)]
                copy = pltpu.make_async_copy(source.at[:, columns(tint, t, away)], out, sems.at[i * 16 + at])
                copy.start()
                copies[i, at] = copy
    for t in range(4):
        at = near_columns(t, 0)
        copies[0, at].wait()
        copies[1, at].wait()
        part = lax.dot_general(near[at], block[t], NT, preferred_element_type=F32)
        total[...] = part if t == 0 else total[...] + part
    for away in range(1, 4):
        for t in range(4):
            for i in range(2):
                copies[i, near_columns(t, away)].wait()


def early_call(tint, head, head_2, block):
    vmem, anywhere = pl.BlockSpec(memory_space=pltpu.VMEM), pl.BlockSpec(memory_space=pl.ANY)
    return pl.pallas_call(
        early_kernel,
        in_specs=[pl.BlockSpec(memory_space=pltpu.SMEM), anywhere, anywhere, vmem],
        out_specs=[vmem] * 2,
        out_shape=[pltpu.VMEM((1024, 256), F32), pltpu.VMEM((16, 1024, 512), BF16)],
        scratch_shapes=[pltpu.SemaphoreType.DMA((32,))],
        cost_estimate=pl.CostEstimate(flops=2 * 1024 * 256 * 2048, bytes_accessed=17 << 20, transcendentals=0),
        compiler_params=pltpu.CompilerParams(vmem_limit_bytes=LIMIT),
    )(
        tint,
        pltpu.with_memory_space_constraint(head, pltpu.HBM),
        pltpu.with_memory_space_constraint(head_2, pltpu.HBM),
        pltpu.with_memory_space_constraint(block, pltpu.VMEM),
    )


def last_kernel(tint, near, block_1, block_2, block_3, early, logits, lse):
    def part(t):
        return sum(
            lax.dot_general(near[near_columns(t, away)], block[t], NT, preferred_element_type=F32)
            for away, block in ((1, block_1), (2, block_2), (3, block_3))
        )

    logits[...] = early[...] + part(0)

    @pl.loop(1, 4)
    def _(t):
        logits[...] += part(t)

    values = logits[...]
    top = jnp.max(values, axis=0, keepdims=True)
    sums = top + jnp.log(jnp.sum(jnp.exp(values - top), axis=0, keepdims=True))
    sums = jnp.concatenate([sums[:, :128], sums[:, 128:]], axis=0)
    lse[...] = jnp.broadcast_to(sums[None], (64, 2, 128))


def last_call(tint, near, blocks, early):
    outs = [((1024, 256), F32, jax.ShapeDtypeStruct), ((64, 2, 128), F32, jax.ShapeDtypeStruct)]
    return call(last_kernel, tint, [near, *blocks, early], outs, 6 * 1024 * 256 * 2048, 17 << 20)


def product(dlogits, near, away, out):
    @pl.loop(0, 4)
    def _(t):
        out[t] = jnp.dot(dlogits[...], near[near_columns(t, away)], preferred_element_type=F32).astype(out.dtype)


def turn_kernel(tint, logits, near, parts, labels, weights, turned, turned_2, dlogits, inner, out, held, sem):
    copy = pltpu.make_async_copy(logits, held, sem)
    copy.start()
    lse = parts[...]
    top = jnp.max(lse, axis=0)
    log_total = top + jnp.log(jnp.sum(jnp.exp(lse - top[None]), axis=0))
    log_total = jnp.concatenate([log_total[:1], log_total[1:]], axis=1)
    copy.wait()
    for i in range(2):
        span = slice(i * 512, (i + 1) * 512)
        probs = jnp.exp(held[span, :] - log_total)
        ids = tint[5 + i] * 512 + lax.broadcasted_iota(jnp.int32, (512, 256), 0)
        hot = jnp.where(ids == labels[...], 1.0, 0.0)
        values = (weights[...] * (probs - hot)).astype(BF16)
        (turned, turned_2)[i][...] = values
        dlogits[:, span] = values.T
        part = jnp.sum(values.astype(F32) * held[span, :], axis=0, keepdims=True)
        inner[...] = part if i == 0 else inner[...] + part
    product(dlogits, near, 1, out)


def turn_call(tint, logits, near, parts, labels, weights):
    vmem = pl.BlockSpec(memory_space=pltpu.VMEM)
    return pl.pallas_call(
        turn_kernel,
        in_specs=[pl.BlockSpec(memory_space=pltpu.SMEM), pl.BlockSpec(memory_space=pl.ANY)] + [vmem] * 4,
        out_specs=[vmem] * 5,
        out_shape=[
            pltpu.VMEM((512, 256), BF16),
            pltpu.VMEM((512, 256), BF16),
            pltpu.VMEM((256, 1024), BF16),
            jax.ShapeDtypeStruct((1, 256), F32),
            pltpu.VMEM((4, 256, 512), BF16),
        ],
        scratch_shapes=[pltpu.VMEM((1024, 256), F32), pltpu.SemaphoreType.DMA],
        cost_estimate=pl.CostEstimate(flops=2 * 1024 * 256 * 2048, bytes_accessed=5 << 20, transcendentals=0),
        compiler_params=pltpu.CompilerParams(vmem_limit_bytes=LIMIT),
    )(tint, logits, pltpu.with_memory_space_constraint(near, pltpu.VMEM), parts, labels, weights)


def back_kernel(away, dlogits, near, out):
    product(dlogits, near, away, out)


def back_call(dlogits, near, away, kind=BF16):
    kernel = functools.partial(back_kernel, away)
    return call(kernel, None, [dlogits, near], [((4, 256, 512), kind)], 2 * 1024 * 256 * 2048, 4 << 20)[0]


def head_kernel(tint, turned, turned_2, *refs):
    out = refs[-1]
    for away in range(4):
        own, other = refs[away], refs[4 + away]
        value = jnp.dot(turned[...], own[0], preferred_element_type=F32)
        value += jnp.dot(turned_2[...], other[0], preferred_element_type=F32)
        out[:, pl.ds(pl.multiple_of(tint[away] * 512, 512), 512)] = value.astype(BF16)


def head_call(tint, turned, turned_2, own, other):
    block = pl.BlockSpec((1, 256, 512), lambda t, tint: (t, 0, 0))
    return pl.pallas_call(
        head_kernel,
        grid_spec=pltpu.PrefetchScalarGridSpec(
            num_scalar_prefetch=1,
            grid=(4,),
            in_specs=[pl.BlockSpec((512, 256), lambda t, tint: (0, 0))] * 2 + [block] * 8,
            out_specs=pl.BlockSpec((512, 2048), lambda t, tint: (0, t)),
        ),
        out_shape=jax.ShapeDtypeStruct((512, 8192), BF16),
        cost_estimate=pl.CostEstimate(flops=2 * 512 * 512 * 8192, bytes_accessed=17 << 20, transcendentals=0),
        compiler_params=pltpu.CompilerParams(vmem_limit_bytes=LIMIT),
    )(tint, turned, turned_2, *own, *other)


def three_parts(value):
    high = value.astype(BF16).astype(F32)
    middle = (value - high).astype(BF16).astype(F32)
    return high, middle, value - high - middle


def join_kernel(came, ours, one, two, three, inner, out, inverse_rms, slots, sems):
    for group in range(16):
        inverse_rms[group * 16 : (group + 1) * 16, :] = jnp.broadcast_to(inverse_of(came, group), (16, 128))
    products = [part[i : i + 1] for part in three_parts(inner[...]) for i in range(2)]
    copies = []
    for t in range(4):
        gain = jnp.zeros((1, 512), F32)
        for group in range(16):
            span = slice(group * 16, (group + 1) * 16)
            total = ours[t, span] + one[t, span].astype(F32) + two[t, span].astype(F32) + three[t, span].astype(F32)
            for i in range(4):
                slots[t * 16 + group, i * 16 : (i + 1) * 16, :] = total[:, i * 128 : (i + 1) * 128].astype(BF16)
            pieces = [came[t * 16 + group, i * 16 : (i + 1) * 16, :] for i in range(4)]
            unit = jnp.concatenate(pieces, axis=1).astype(F32) * inverse_rms[span, :1]
            gain += jnp.sum(total * unit, axis=0, keepdims=True)
        high, middle, _ = three_parts(gain)
        for share in range(8):
            part = jnp.concatenate([p[:, share * 64 : (share + 1) * 64] for p in (high, middle)], axis=1)
            extra = jnp.concatenate([part] + products + [jnp.zeros((1, 128), F32)], axis=0).astype(BF16)
            slots[t * 16 + share * 2, 64:, :] = extra
            slots[t * 16 + share * 2 + 1, 64:, :] = extra
        span = pl.ds(t * 16, 16)
        copies.append(pltpu.make_async_copy(slots.at[span], out.at[span], sems.at[t]))
        copies[-1].start()
    for copy in copies:
        copy.wait()


def join_call(*operands):
    vmem = pl.BlockSpec(memory_space=pltpu.VMEM)
    return pl.pallas_call(
        join_kernel,
        in_specs=[vmem] * len(operands),
        out_specs=[pl.BlockSpec(memory_space=pl.ANY), vmem],
        out_shape=[pltpu.HBM((64, 72, 128), BF16), pltpu.VMEM((256, 128), F32)],
        scratch_shapes=[pltpu.VMEM((64, 72, 128), BF16), pltpu.SemaphoreType.DMA((4,))],
        cost_estimate=pl.CostEstimate(flops=0, bytes_accessed=6 << 20, transcendentals=0),
        compiler_params=pltpu.CompilerParams(vmem_limit_bytes=LIMIT),
    )(*[pltpu.with_memory_space_constraint(o, pltpu.VMEM) for o in operands])


def tail_kernel(info, terms, rows, inverse_rms, gain, placed):
    sums, extra = [[None] * 4 for _ in range(4)], [None] * 4
    for chip, colour in enumerate(COLOURS):
        for i in range(4):
            term = terms[chip, i * 16 : (i + 1) * 16, :].astype(F32)
            sums[colour][i] = term if sums[colour][i] is None else sums[colour][i] + term
        term = terms[chip, 64:, :].astype(F32)
        extra[colour] = term if extra[colour] is None else extra[colour] + term
    products = sum(extra)[1:7]
    lane = lax.broadcasted_iota(jnp.int32, (16, 128), 1)
    row = info[2] * 16 + lax.broadcasted_iota(jnp.int32, (16, 128), 0)
    here = [jnp.where(lane + 128 * (i % 2) == row, products[i : i + 1], 0.0) for i in range(6)]
    inner = jnp.sum(sum(here), axis=1, keepdims=True) / 8192
    inverse = inverse_rms[:, :1]
    share = jnp.concatenate([e[:1, :64] + e[:1, 64:] for e in extra], axis=1)
    parts = [part[:, i * 128 : (i + 1) * 128] for part in three_parts(share)[:2] for i in range(2)]
    beside = jnp.concatenate(parts + [jnp.zeros((4, 128), F32)], axis=0).astype(BF16)
    for section in range(16):
        placed[section, :, 2048:] = beside
    for colour in range(4):
        span = slice(colour * 512, (colour + 1) * 512)
        unit = rows[:, span].astype(F32) * inverse
        total = jnp.concatenate(sums[colour], axis=1)
        exit_grad = inverse * (total * gain[:, span] - unit * inner)
        for section in range(16):
            value = jnp.where(info[0] == section, exit_grad[:8], jnp.where(info[1] == section, exit_grad[8:], 0.0))
            placed[section, :, span] = value.astype(BF16)


def tail_call(info, *operands):
    outs = [((16, 8, 2176), BF16, True)]
    return call(tail_kernel, info, operands, outs, moved=2 << 20)[0]


def hold_kernel(source, out):
    out[...] = source[...]


def add_kernel(exits, from_next, out):
    out[...] = (exits[:, :, :2048].astype(F32) + from_next[...].astype(F32)).astype(BF16)


def local(hidden, section_cotangent, norm_gain, head, labels, loss_mask, exit_on):
    core, x, y, zl, zh = (lax.axis_index(a) for a in ("c", "x", "y", "zl", "zh"))
    device = lax.axis_index(AXES).astype(jnp.int32)
    colour = (x + 2 * y + 3 * (2 * zh + zl)) % 4
    aways = (colour + jnp.arange(4, dtype=jnp.int32)) % 4
    tint = jnp.concatenate([aways, core.reshape(1), device.reshape(1), (device + 8 - 16 * core).reshape(1)]).astype(jnp.int32)

    head_2 = other_core(head)
    came = lax.all_to_all(hidden.reshape(16, 8, 2048), PIPE, 0, 0, tiled=True)
    section_ids = jnp.arange(16, dtype=jnp.int32)
    first = jnp.min(jnp.where(exit_on == 1, section_ids, 16))
    second = jnp.max(jnp.where(exit_on == 1, section_ids, -1))
    chosen = jnp.stack([first, second])
    scores = (chosen + 1).astype(F32)
    weights = scores / jnp.sum(scores)

    rows = jnp.concatenate([lax.dynamic_index_in_dim(came, s, 0, False) for s in (first, second)])
    norm_gain, rows = lax.optimization_barrier((norm_gain, rows))
    turns = [norm_gain] + [move(norm_gain, lambda y, z, c, x, k=k: (y, z, c, x + k)) for k in (1, 2, 3)]
    ring = jnp.stack(turns[::-1] * 2)
    gain = lax.dynamic_slice(ring, ((3 - x) % 4, colour * 512), (4, 512))
    token_info, rows = lax.optimization_barrier((jnp.stack([labels, loss_mask]), rows))
    other_info = move(token_info, lambda y, z, c, x: (y, z + 2, c, x))
    both = jnp.where(zh == 0, jnp.stack([token_info, other_info]), jnp.stack([other_info, token_info]))
    by_row = jnp.broadcast_to(
        both.reshape(2, 2, 4, 2, 2, 8).transpose(4, 1, 2, 3, 0, 5)[:, :, :, :, :, None], (2, 2, 4, 2, 2, 2, 8)
    )
    by_row = jnp.where(core == 0, by_row[0], by_row[1])
    row_labels = by_row[0].reshape(1, 256)
    row_weights = (weights[:, None] * by_row[1].astype(F32)).reshape(1, 256)

    quarter = lax.all_to_all(slots_call(rows), CHIPS, 0, 0, tiled=True)
    quarter, row_labels, row_weights, gain = lax.optimization_barrier((quarter, row_labels, row_weights, gain))
    own = norm_call(quarter, gain)

    blocks = [own, to_colour(own, 3), to_colour(own, 2), to_colour(own, 1)]
    early, near = early_call(tint, head, head_2, own)
    *blocks[1:], early = lax.optimization_barrier((*blocks[1:], early))
    logits, lse = last_call(tint, near, blocks[1:], early)
    parts = lax.all_to_all(lse, CHIPS, 0, 0, tiled=True)
    turned, turned_2, dlogits, inner, product_1 = turn_call(tint, logits, near, parts, row_labels, row_weights)

    sums = [product_1] + [back_call(dlogits, near, away) for away in (2, 3)]
    arrived = [to_colour(s, away) for s, away in zip(sums, (1, 2, 3))]
    late, _ = lax.optimization_barrier((dlogits, sums[2]))
    ours = back_call(late, near, 0, F32)
    turned_2 = other_core(turned_2)
    ours, turned_2, *blocks = lax.optimization_barrier((ours, turned_2, *blocks))
    mates = [other_core(b) for b in blocks]
    inner = inner.reshape(2, 128)
    slots, inverse_rms = join_call(quarter, ours, *arrived, inner)
    terms = lax.all_to_all(slots, CHIPS, 0, 0, tiled=True)
    head_grad = head_call(tint, turned, turned_2, blocks, mates)
    place = (y * 2 + zl) * 2 + zh
    inverse_here = lax.dynamic_slice_in_dim(inverse_rms, place * 16, 16, 0)
    terms, head_grad, inverse_here = lax.optimization_barrier((terms, head_grad, inverse_here))
    info = jnp.concatenate([chosen, place.reshape(1)]).astype(jnp.int32)
    placed = tail_call(info, terms, rows, inverse_here, norm_gain.reshape(1, 2048))
    came = lax.all_to_all(placed, PIPE, 0, 0, tiled=True)
    from_next = move(section_cotangent, back_one)
    from_next = call(hold_kernel, None, [from_next.reshape(16, 8, 2048)], [((16, 8, 2048), BF16)])[0]
    residual_grad = call(add_kernel, None, [came, from_next], [((16, 8, 2048), BF16, True)])[0].reshape(1, 128, 2048)
    came, residual_grad = lax.optimization_barrier((came, residual_grad))
    shares = came[:, :4, 2048:].astype(F32).reshape(8, 2, 2, 4, 64)
    gain_grad = jnp.sum(shares, axis=(1, 2)).transpose(1, 0, 2).reshape(2048)
    return head_grad, residual_grad, gain_grad


def solution(mesh):
    fine = Mesh(mesh.devices.reshape(SIZES), AXES)
    in_specs = (
        P(PIPE, "zh", "x"),
        P(PIPE, "zh", "x"),
        P("x"),
        P(AXES, None),
        P("zh"),
        P("zh"),
        P(),
    )
    out_specs = (P(AXES, None), P(PIPE, "zh", "x"), P("x"))
    return jax.shard_map(local, mesh=fine, in_specs=in_specs, out_specs=out_specs, check_vma=False)
```
